512 devices in a mesh: tm: 16 (over y, x), space: 32 (over z, core).
Axes of the slice: x: 4, y: 4, z: 16, core: 2. Of those that a mesh axis runs over, the one named last changes fastest.
Arguments:
- video: float32 [32, 64, 32, 256], P('tm', 'space'), may hold values from -6 to 6
- clip_ids: int32 [32], replicated, may hold values from 0 to 9, never falling along the last dimension, each value on 1 to 4 neighbouring positions
- norm1_gain: float32 [256], replicated, may hold values from 0.1 to 1.9
- conv1_weight: float32 [3, 3, 3, 256, 256], P(None, None, None, 'tm'), may hold values from -0.078125 to 0.078125
- norm2_gain: float32 [256], replicated, may hold values from 0.1 to 1.9
- conv2_weight: float32 [3, 3, 3, 256, 256], P(None, None, None, 'tm'), may hold values from -0.078125 to 0.078125
- norm3_gain: float32 [256], replicated, may hold values from 0.1 to 1.9
- qk_weight: float32 [2, 256, 256], replicated, may hold values from -40 to 40
- value_weight: float32 [256, 256], replicated, may hold values from -0.375 to 0.375
- proj_weight: float32 [256, 256], replicated, may hold values from -0.375 to 0.375
Outputs:
- encoded: float32 [32, 64, 32, 256], P('tm', 'space')
The draws below stay inside these ranges and needn't reach their ends.
Inputs may be any that keep to these rules, and one draw needn't show every extreme that they name: clip_ids never falls; each clip has 1 to 4 consecutive frames, and one has exactly 4.
All inputs are finite; a program needn't handle non-finite values.
Results may differ from the reference program's by a relative error of at most 0.0003.
Values sent between devices are 32-bit elements; how exact they have to be, the bound alone decides.
No kernel may reach another device: no remote copies, remote signals or barrier semaphores. Data moves between devices by JAX's collectives and lax.ppermute only.
A program may use at most 64 MiB of HBM per device.

```python
import math
import jax
import jax.numpy as jnp
import numpy as np
from jax import lax

C = 256
COLS = 32
CLIP_MOST = 4
CLIPS = 10
FRAMES = 32
ROWS = 64


def draw_qk_weight(key, part):
    key = jax.random.fold_in(key, 7)
    first_key, second_key = jax.random.split(key, 2)
    base = jax.random.truncated_normal(first_key, -4.0, 4.0, (C, C), jnp.float32) / math.sqrt(C)
    other = jax.random.truncated_normal(second_key, -4.0, 4.0, (C, C), jnp.float32) / math.sqrt(C)
    query_part = base
    key_part = other
    return jnp.stack([query_part, key_part])


def block_scale(rng, dims, cuts, low, top_value):
    loudness = 1.0
    for dim, blocks in cuts:
        draws = jax.random.uniform(jax.random.fold_in(jax.random.fold_in(rng, 6), dim), (blocks,), jnp.float32, low / len(cuts), top_value / len(cuts))
        loudness = loudness * jnp.repeat(jnp.exp(draws), dims[dim] // blocks).reshape((-1,) + (1,) * (len(dims) - 1 - dim))
    return loudness


def length_profile(count, total, most, skew):
    portions = [(1 << 20) // math.isqrt(grade ** skew) + 1 for grade in range(2, count + 1)]
    spare, given = total - most - (count - 1), [1] * (count - 1)
    while spare > 0:
        movable = [i for i in range(count - 1) if given[i] < most]
        whole, remaining = sum([portions[i] for i in movable]), spare
        for i in movable:
            extra = min(most - given[i], max(1, remaining * portions[i] // whole), spare)
            given[i] = given[i] + extra
            spare = spare - extra
    return np.array([most] + given)


def ragged(key, number_of, total, reach, skew):
    if number_of == 2:
        one = jax.random.randint(key, (), max(1, total - reach), min(reach, total - 1) + 1)
        return jnp.stack([one, total - one])
    tallies = jnp.asarray(length_profile(number_of, total, reach, skew), jnp.int32)
    pairs = (number_of - 1) // 2
    giver, receiver = tallies[1:1 + 2 * pairs:2], tallies[2:2 + 2 * pairs:2]
    slack = jnp.minimum(giver - 1, reach - receiver)
    moved = jax.random.randint(jax.random.fold_in(key, 1), (pairs,), 0, 1 << 20) % (slack + 1)
    tallies = tallies.at[1:1 + 2 * pairs:2].set(giver - moved).at[2:2 + 2 * pairs:2].set(receiver + moved)
    return tallies[jax.random.permutation(jax.random.fold_in(key, 2), number_of)]


def normal_values(own_key, extent, deviation, most, cuts=(), kind=jnp.bfloat16):
    drawn = deviation * jax.random.normal(own_key, extent, jnp.float32)
    if cuts:
        drawn = drawn * block_scale(own_key, extent, cuts, -0.22, 0.18)
    return jnp.clip(drawn, -most, most).astype(kind)


def setup_inputs(seed: int = 0) -> dict:
    keys = jax.random.split(jax.random.key(seed), 11)
    video = normal_values(keys[0], (FRAMES, ROWS, COLS, C), 1.0, 6.0, ((0, 16), (1, 32)), jnp.float32)
    clip_ids = jnp.searchsorted(jnp.cumsum(ragged(keys[1], CLIPS, FRAMES, CLIP_MOST, 0)), jnp.arange(FRAMES), side="right").astype(jnp.int32)
    norm1_gain = jnp.clip(1.0 + 0.18 * jax.random.normal(keys[2], (C,), jnp.float32), 0.1, 1.9)
    conv1_weight = normal_values(keys[3], (3, 3, 3, C, C), (27 * C) ** -0.5, 0.078125, ((3, 16),), jnp.float32)
    norm2_gain = jnp.clip(1.0 + 0.18 * jax.random.normal(keys[4], (C,), jnp.float32), 0.1, 1.9)
    conv2_weight = normal_values(keys[5], (3, 3, 3, C, C), (27 * C) ** -0.5, 0.078125, ((3, 16),), jnp.float32)
    norm3_gain = jnp.clip(1.0 + 0.18 * jax.random.normal(keys[6], (C,), jnp.float32), 0.1, 1.9)
    qk_weight = draw_qk_weight(jax.random.fold_in(keys[10], 71), 0)
    value_weight = normal_values(keys[8], (C, C), C ** -0.5, 0.375, (), jnp.float32)
    proj_weight = normal_values(keys[9], (C, C), C ** -0.5, 0.375, (), jnp.float32)
    return dict(video=video, clip_ids=clip_ids, norm1_gain=norm1_gain, conv1_weight=conv1_weight, norm2_gain=norm2_gain, conv2_weight=conv2_weight, norm3_gain=norm3_gain, qk_weight=qk_weight, value_weight=value_weight, proj_weight=proj_weight)


highest = lax.Precision.HIGHEST
epsilon = 1e-06

def rms_scale(volume, gain_vec):
    return volume * lax.rsqrt(lax.optimization_barrier(jnp.mean(volume * volume, axis=-1, keepdims=True)) + epsilon) * gain_vec

def causal_conv(volume, clip_ids, weight):
    frames, height, breadth = (volume.shape[0], volume.shape[1], volume.shape[2])
    padded = jnp.pad(volume, ((2, 0), (1, 1), (1, 1), (0, 0)))
    padded_ids = jnp.concatenate([jnp.full((2,), -1, jnp.int32), clip_ids.astype(jnp.int32)])
    summed = jnp.zeros((frames, height, breadth, weight.shape[3]), jnp.float32)
    for tap_t in range(3):
        same_clip = (padded_ids[tap_t:tap_t + frames] == clip_ids.astype(jnp.int32)).astype(jnp.float32)
        for tap_y in range(3):
            for tap_x in range(3):
                window = padded[tap_t:tap_t + frames, tap_y:tap_y + height, tap_x:tap_x + breadth]
                product = jnp.einsum('fhwc,dc->fhwd', window, weight[tap_t, tap_y, tap_x], precision=highest)
                summed = summed + same_clip[:, None, None, None] * product
    return summed

def frame_attention(frame_tokens, query_weight, key_weight, value_weight):
    queries = jnp.dot(frame_tokens, query_weight, precision=highest)
    keys_all = jnp.dot(frame_tokens, key_weight, precision=highest)
    values = jnp.dot(frame_tokens, value_weight, precision=highest)
    scores = jnp.dot(queries, keys_all.T, precision=highest) / math.sqrt(frame_tokens.shape[-1])
    return jnp.dot(jax.nn.softmax(scores, axis=-1), values, precision=highest)

def reference(video, clip_ids, norm1_gain, conv1_weight, norm2_gain, conv2_weight, norm3_gain, qk_weight, value_weight, proj_weight):
    inner = jax.nn.silu(rms_scale(video, norm1_gain))
    inner = causal_conv(inner, clip_ids, conv1_weight)
    inner = jax.nn.silu(rms_scale(inner, norm2_gain))
    inner = causal_conv(inner, clip_ids, conv2_weight)
    blocked = video + inner
    normed = rms_scale(blocked, norm3_gain)
    frames, height, breadth, channels = normed.shape
    tokens = normed.reshape(frames, height * breadth, channels)
    attended = lax.map(lambda frame_tokens: frame_attention(frame_tokens, qk_weight[0], qk_weight[1], value_weight), tokens)
    projected = jnp.dot(attended, proj_weight, precision=highest)
    return blocked + projected.reshape(frames, height, breadth, channels)
```

```python
import math

import jax
import jax.numpy as jnp
from jax import lax
from jax.experimental import pallas as pl
from jax.experimental.pallas import tpu as pltpu
from jax.sharding import Mesh
from jax.sharding import PartitionSpec as P

highest = lax.Precision.HIGHEST
epsilon = 1e-06
f32 = jnp.float32
bf16 = jnp.bfloat16

Y, X, K, L, CORES = 4, 4, 8, 2, 2
SPACE = K * L * CORES
OFFSETS = ((0, 8), (2, -2), (4, -4), (6, -6))

VMEM_LIMIT = 48 * 1024 * 1024


def call(kernel, out_shape, scratch, *operands, smem=0):
    return pl.pallas_call(
        kernel,
        out_shape=out_shape,
        in_specs=[pl.BlockSpec(memory_space=pltpu.SMEM)] * smem
        + [pl.BlockSpec(memory_space=pltpu.VMEM)] * (len(operands) - smem),
        out_specs=jax.tree.map(lambda _: pl.BlockSpec(memory_space=pltpu.VMEM), out_shape),
        scratch_shapes=scratch,
        compiler_params=pltpu.CompilerParams(vmem_limit_bytes=VMEM_LIMIT),
    )(*operands)


def shape(*dims):
    return jax.ShapeDtypeStruct(dims, f32)


def column(gain_row):
    return jnp.broadcast_to(gain_row, (128, gain_row.shape[1])).T


def split(value):
    high = value.astype(bf16)
    return high, (value - high.astype(f32)).astype(bf16)


def dot3(a_high, a_low, b_high, b_low, dims=((1,), (0,))):
    def one(a, b):
        return lax.dot_general(a, b, (dims, ((), ())), preferred_element_type=f32)

    return one(a_high, b_low) + one(a_low, b_high) + one(a_high, b_high)


def norm_silu(value, gain):
    scale = lax.rsqrt(jnp.mean(value * value, axis=0, keepdims=True) + epsilon)
    value = value * scale * gain
    return value / (1.0 + jnp.exp(-value))


def lanes():
    lane = lax.broadcasted_iota(jnp.int32, (16, 128), 1)
    return lane, lane % 32, (lane // 32) % 2


def taps(product):
    _, across, row = lanes()
    left, right, first_row = across >= 1, across <= 30, row == 0
    result = []
    for a in range(3):
        rows = []
        for b in range(3):
            base = (a * 9 + b * 3) * 16
            rows.append(
                product[base + 16 : base + 32]
                + jnp.where(left, pltpu.roll(product[base : base + 16], 1, 1), 0.0)
                + jnp.where(right, pltpu.roll(product[base + 32 : base + 48], 127, 1), 0.0)
            )
        stay = jnp.where(first_row, rows[0], rows[2])
        own = rows[1] + jnp.where(first_row, pltpu.roll(stay, 96, 1), pltpu.roll(stay, 32, 1))
        leave = jnp.where(first_row, rows[2], rows[0])
        result.append(jnp.concatenate([own, leave], axis=0))
    return result


def in_time(now, before, mask_1, mask_2):
    lane = lax.broadcasted_iota(jnp.int32, (32, 128), 1)
    pair = jnp.where(lane < 64, now[1], before[1])
    return now[2] + mask_1 * pltpu.roll(pair, 64, 1) + mask_2 * before[0]


def spread_kernel(video_ref, out_ref):
    flipped = video_ref[...].T
    for i in range(Y * X):
        out_ref[i] = flipped


def conv1_kernel(
    place_ref, video_ref, weight_ref, gain_ref, mask_ref, own_ref, up_ref, down_ref, kept_ref
):
    _, _, row = lanes()
    first_row = row == 0
    gain = column(gain_ref[...])
    w_high, w_low = split(weight_ref[...])
    kept_ref[...] = video_ref[pl.ds(4 * place_ref[0], 4), :, place_ref[1]]

    def step(p, before):
        pieces = []
        for half in range(2):
            tile = video_ref[2 * p + half].reshape(256, 128)
            pieces.append(split(norm_silu(tile, gain)))
        high = jnp.concatenate([pieces[0][0], pieces[1][0]], axis=1)
        low = jnp.concatenate([pieces[0][1], pieces[1][1]], axis=1)
        product = dot3(w_high, w_low, high, low)
        outside = []
        for half in range(2):
            j = 2 * p + half
            now = taps(product[:, 128 * half : 128 * half + 128])
            done = in_time(now, before, mask_ref[0, pl.ds(j, 1)], mask_ref[1, pl.ds(j, 1)])
            own_ref[j] = done[:16]
            outside.append(done[16:])
            before = now
        up_ref[p] = jnp.where(first_row, outside[0], pltpu.roll(outside[1], 32, 1))
        down_ref[p] = jnp.where(first_row, pltpu.roll(outside[0], 96, 1), outside[1])
        return before

    zero = jnp.zeros((32, 128), f32)
    lax.fori_loop(0, 8, step, [zero, zero, zero])


def join1_kernel(own_ref, from_above_ref, from_below_ref, out_ref):
    _, _, row = lanes()
    first_row = row == 0
    out_ref[0:4, 0] = jnp.zeros((4, 16, 128), f32)
    for p in range(8):
        above, below = from_above_ref[p], from_below_ref[p]
        added = (
            jnp.where(first_row, above, pltpu.roll(below, 32, 1)),
            jnp.where(first_row, pltpu.roll(above, 96, 1), below),
        )
        for half in range(2):
            j = 2 * p + half
            tile = own_ref[j] + added[half]
            y, q = j // 4, j % 4
            for x in range(X):
                out_ref[4 * y + x, q + 1] = tile
                if q == 3 and y < 3:
                    out_ref[4 * (y + 1) + x, 0] = tile


def conv2_kernel(
    place_ref, second_ref, weight_ref, gain_ref, mask_ref, kept_ref, out_ref, high_ref, low_ref
):
    lane, _, _ = lanes()
    low_half = lane < 64
    gain = column(gain_ref[...])
    for q in range(5):
        tile = second_ref[:, q].reshape(256, 128)
        high, low = split(norm_silu(tile, gain))
        high_ref[:, 128 * q : 128 * q + 128] = high
        low_ref[:, 128 * q : 128 * q + 128] = low
    first = 4 * place_ref[0]

    def step(g, _):
        w_high, w_low = split(weight_ref[g])
        product = dot3(w_high, w_low, high_ref[...], low_ref[...])
        before = taps(product[:, :128])
        for q in range(4):
            now = taps(product[:, 128 * (q + 1) : 128 * (q + 2)])
            done = in_time(
                now, before, mask_ref[0, pl.ds(first + q, 1)], mask_ref[1, pl.ds(first + q, 1)]
            )
            own = done[:16] + kept_ref[q, g]
            leave = done[16:]
            out_ref[q, g] = jnp.where(low_half, own, pltpu.roll(leave, 64, 1))
            out_ref[q + 4, g] = jnp.where(low_half, pltpu.roll(own, 64, 1), leave)
            before = now
        return 0

    lax.fori_loop(0, 4, step, 0)


def join2_kernel(parts_ref, out_ref):
    lane, _, _ = lanes()
    first_row, low_half = lane < 32, lane < 64
    zero = jnp.zeros((16, 128), f32)

    def band(s):
        above = parts_ref[s - 1] if s > 0 else zero
        below = parts_ref[s + 1] if s < SPACE - 1 else zero
        return parts_ref[s] + jnp.where(
            first_row, pltpu.roll(above, 32, 1), pltpu.roll(below, 96, 1)
        )

    for p in range(16):
        tile = jnp.where(low_half, band(2 * p), pltpu.roll(band(2 * p + 1), 64, 1))
        for i in range(X * L):
            out_ref[i, p] = tile


def attend_kernel(
    place_ref, mine_ref, other_ref, gain_ref, qk_ref, value_ref, proj_ref, out_ref,
    blocked_ref, normed_ref, high_ref, low_ref,
):
    gain = column(gain_ref[...])
    even = place_ref[2] == 0
    for p in range(16):
        mine, other = mine_ref[:, p], other_ref[:, p]
        on_0 = jnp.where(even, mine, other)
        on_1 = jnp.where(even, other, mine)
        blocks = []
        for l in range(L):
            for part in (on_0, on_1):
                blocks += [part[2 * x + l] for x in range(X)]
        tile = jnp.concatenate(blocks, axis=0)
        blocked_ref[p] = tile
        normed = tile * lax.rsqrt(jnp.mean(tile * tile, axis=0, keepdims=True) + epsilon) * gain
        normed_ref[:, 128 * p : 128 * p + 128] = normed
        high, low = split(normed)
        high_ref[:, 128 * p : 128 * p + 128] = high
        low_ref[:, 128 * p : 128 * p + 128] = low
    at = place_ref[3]
    rows = blocked_ref[at].T
    normed_rows = rows * lax.rsqrt(jnp.mean(rows * rows, axis=1, keepdims=True) + epsilon) * gain_ref[...]
    queries = jnp.dot(normed_rows, qk_ref[0], precision=highest, preferred_element_type=f32)
    queries = lax.dot_general(
        queries, qk_ref[1], (((1,), (1,)), ((), ())), precision=highest, preferred_element_type=f32
    ) * (1.0 / math.sqrt(256))
    scores = jnp.dot(queries, normed_ref[...], precision=highest, preferred_element_type=f32)
    weights = jnp.exp(scores - jnp.max(scores, axis=1, keepdims=True))
    total = jnp.sum(weights, axis=1, keepdims=True)
    e_high, e_low = split(weights)
    attended = dot3(e_high, e_low, high_ref[...], low_ref[...], ((1,), (1,))) / total
    attended = jnp.dot(attended, value_ref[...], precision=highest, preferred_element_type=f32)
    attended = jnp.dot(attended, proj_ref[...], precision=highest, preferred_element_type=f32)
    result = rows + attended
    swapped = place_ref[4]
    out_ref[swapped] = result[:64]
    out_ref[1 - swapped] = result[64:]


def delivery():
    routes = ([], [])
    for x in range(X):
        for k in range(K):
            for l in range(L):
                for c in range(CORES):
                    source = ((x * K + k) * L + l) * CORES + c
                    chip = (2 * k + l + OFFSETS[x][c]) % (K * L)
                    f = k // 4
                    for route, core in zip(routes, (f, 1 - f)):
                        route.append((source, ((k % 4) * K * L + chip) * CORES + core))
    return routes


def body(
    video,
    clip_ids,
    norm1_gain,
    conv1_weight,
    norm2_gain,
    conv2_weight,
    norm3_gain,
    qk_weight,
    value_weight,
    proj_weight,
):
    space = ("k", "l", "c")
    y, x, k, l, c = (lax.axis_index(n) for n in ("y", "x", "k", "l", "c"))
    offset = jnp.where(c == 0, jnp.where(x == 0, 0, 2 * x), jnp.where(x == 0, 8, -2 * x))
    place = jnp.stack([y, x, c, (2 * k + l + offset) % (K * L), k // 4]).astype(jnp.int32)

    earlier = jnp.concatenate([jnp.full((2,), -1, jnp.int32), clip_ids])
    same = jnp.stack([earlier[1:-1] == clip_ids, earlier[:-2] == clip_ids]).astype(f32)
    masks = jnp.repeat(same, 64, axis=1).reshape(2, 16, 128)

    weight_2 = lax.all_gather(conv2_weight.reshape(432, 256), "y", axis=0)

    spread = call(spread_kernel, shape(Y * X, 256, 128), [], video.reshape(128, 256))
    everywhere = lax.all_to_all(spread, ("y", "x"), 0, 0)
    own, up, down, kept = call(
        conv1_kernel,
        [shape(16, 16, 128), shape(8, 16, 128), shape(8, 16, 128), shape(4, Y, 16, 128)],
        [],
        place,
        everywhere.reshape(16, Y, X, 16, 128),
        conv1_weight.reshape(432, 256),
        norm1_gain.reshape(1, 256),
        masks,
        smem=1,
    )
    onward = [(i, i + 1) for i in range(SPACE - 1)]
    from_above = lax.ppermute(down, space, onward)
    from_below = lax.ppermute(up, space, [(j, i) for i, j in onward])
    second = call(join1_kernel, shape(Y * X, 5, 16, 128), [], own, from_above, from_below)
    second = lax.all_to_all(second, ("y", "x"), 0, 0)
    parts = call(
        conv2_kernel,
        shape(K, 4, 16, 128),
        [pltpu.VMEM((256, 640), bf16)] * 2,
        place,
        second,
        weight_2,
        norm2_gain.reshape(1, 256),
        masks,
        kept,
        smem=1,
    )
    parts = lax.all_to_all(parts.reshape(SPACE, 16, 128), space, 0, 0)
    frame = call(join2_kernel, shape(X * L, 16, 16, 128), [], parts)
    mine = lax.all_to_all(frame, ("x", "l"), 0, 0)
    other = lax.ppermute(mine, "c", [(0, 1), (1, 0)])
    encoded = call(
        attend_kernel,
        shape(2, 64, 256),
        [
            pltpu.VMEM((16, 256, 128), f32),
            pltpu.VMEM((256, 2048), f32),
            pltpu.VMEM((256, 2048), bf16),
            pltpu.VMEM((256, 2048), bf16),
        ],
        place,
        mine,
        other,
        norm3_gain.reshape(1, 256),
        qk_weight,
        value_weight,
        proj_weight,
        smem=1,
    )
    route_0, route_1 = delivery()
    same_core = lax.ppermute(encoded[0], ("x", "k", "l", "c"), route_0)
    other_core = lax.ppermute(encoded[1], ("x", "k", "l", "c"), route_1)
    first_frame = jnp.where(c == 0, same_core, other_core)
    second_frame = jnp.where(c == 0, other_core, same_core)
    return jnp.stack([first_frame, second_frame]).reshape(video.shape)


def solution(mesh):
    grid = Mesh(mesh.devices.reshape(Y, X, K, L, CORES), ("y", "x", "k", "l", "c"))
    tm, space = ("y", "x"), ("k", "l", "c")
    in_specs = (
        P(tm, space, None, None),
        P(),
        P(),
        P(None, None, None, tm, None),
        P(),
        P(None, None, None, tm, None),
        P(),
        P(),
        P(),
        P(),
    )
    return jax.shard_map(
        body, mesh=grid, in_specs=in_specs, out_specs=P(tm, space, None, None), check_vma=False
    )
```

```python
import math

import jax
import jax.numpy as jnp
from jax import lax
from jax.experimental import pallas as pl
from jax.experimental.pallas import tpu as pltpu
from jax.sharding import Mesh
from jax.sharding import PartitionSpec as P

highest = lax.Precision.HIGHEST
epsilon = 1e-06
f32 = jnp.float32
bf16 = jnp.bfloat16

H, W, X, K, L, CORES = 2, 2, 4, 8, 2, 2
SPACE = K * L * CORES
OFFSETS = ((0, 8), (2, -2), (4, -4), (6, -6))

VMEM_LIMIT = 48 * 1024 * 1024


def call(kernel, out_shape, scratch, *operands, smem=0):
    return pl.pallas_call(
        kernel,
        out_shape=out_shape,
        in_specs=[pl.BlockSpec(memory_space=pltpu.SMEM)] * smem
        + [pl.BlockSpec(memory_space=pltpu.VMEM)] * (len(operands) - smem),
        out_specs=jax.tree.map(lambda _: pl.BlockSpec(memory_space=pltpu.VMEM), out_shape),
        scratch_shapes=scratch,
        compiler_params=pltpu.CompilerParams(vmem_limit_bytes=VMEM_LIMIT),
    )(*operands)


def shape(*dims):
    return jax.ShapeDtypeStruct(dims, f32)


def column(gain_row):
    return jnp.broadcast_to(gain_row, (128, gain_row.shape[1])).T


def split(value):
    high = value.astype(bf16)
    return high, (value - high.astype(f32)).astype(bf16)


def dot3(a_high, a_low, b_high, b_low, dims=((1,), (0,))):
    def one(a, b):
        return lax.dot_general(a, b, (dims, ((), ())), preferred_element_type=f32)

    return one(a_high, b_low) + one(a_low, b_high) + one(a_high, b_high)


def norm_silu(value, gain):
    scale = lax.rsqrt(jnp.mean(value * value, axis=0, keepdims=True) + epsilon)
    value = value * scale * gain
    return value / (1.0 + jnp.exp(-value))


def lanes():
    lane = lax.broadcasted_iota(jnp.int32, (16, 128), 1)
    return lane, lane % 32, (lane // 32) % 2


def taps(product):
    _, across, row = lanes()
    left, right, first_row = across >= 1, across <= 30, row == 0
    result = []
    for a in range(3):
        rows = []
        for b in range(3):
            base = (a * 9 + b * 3) * 16
            rows.append(
                product[base + 16 : base + 32]
                + jnp.where(left, pltpu.roll(product[base : base + 16], 1, 1), 0.0)
                + jnp.where(right, pltpu.roll(product[base + 32 : base + 48], 127, 1), 0.0)
            )
        stay = jnp.where(first_row, rows[0], rows[2])
        own = rows[1] + jnp.where(first_row, pltpu.roll(stay, 96, 1), pltpu.roll(stay, 32, 1))
        leave = jnp.where(first_row, rows[2], rows[0])
        result.append(jnp.concatenate([own, leave], axis=0))
    return result


def in_time(now, before, mask_1, mask_2):
    lane = lax.broadcasted_iota(jnp.int32, (32, 128), 1)
    pair = jnp.where(lane < 64, now[1], before[1])
    return now[2] + mask_1 * pltpu.roll(pair, 64, 1) + mask_2 * before[0]


def spread_kernel(video_ref, out_ref):
    flipped = video_ref[...].T
    for i in range(W * X):
        out_ref[i] = flipped


def conv1_kernel(
    place_ref, video_ref, weight_ref, partner_ref, gain_ref, mask_ref,
    own_ref, beside_ref, beyond_ref, kept_ref, high_ref, low_ref, product_ref,
):
    _, _, row = lanes()
    first_row = row == 0
    gain = column(gain_ref[...])
    for g, ref in enumerate((weight_ref, partner_ref)):
        high_ref[g], low_ref[g] = split(ref[...])
    half, across, core = place_ref[0], place_ref[2], place_ref[3]
    kept_ref[...] = video_ref[pl.ds(4 * place_ref[1], 4), :, across]

    def finish(j, now, before):
        masks = mask_ref[0, pl.ds(8 * half + j, 1)], mask_ref[1, pl.ds(8 * half + j, 1)]
        outside = []
        for g in range(2):
            done = in_time(now[g], before[g], *masks)
            own_ref[j, half if g == 0 else 1 - half] = done[:16]
            outside.append(done[16:])
        up = jnp.where(first_row, outside[0], pltpu.roll(outside[1], 32, 1))
        down = jnp.where(first_row, pltpu.roll(outside[0], 96, 1), outside[1])
        on_even = core == 0
        beside_ref[j] = jnp.where(on_even, down, up)
        beyond_ref[j] = jnp.where(on_even, up, down)

    def step(p, before):
        pieces = []
        for side in range(2):
            tile = video_ref[2 * p + side].reshape(256, 128)
            pieces.append(split(norm_silu(tile, gain)))
        high = jnp.concatenate([pieces[0][0], pieces[1][0]], axis=1)
        low = jnp.concatenate([pieces[0][1], pieces[1][1]], axis=1)
        for g in range(2):
            product_ref[g] = dot3(high_ref[g], low_ref[g], high, low)
        for side in range(2):
            now = [taps(product_ref[g, :, 128 * side : 128 * side + 128]) for g in range(2)]
            finish(2 * p + side, now, before)
            before = now
        return before

    zeros = [[jnp.zeros((32, 128), f32)] * 3] * 2
    last = lax.fori_loop(0, 4, step, zeros)
    finish(8, zeros, last)


def join1_kernel(place_ref, own_ref, beside_ref, beyond_ref, out_ref, history_ref):
    _, _, row = lanes()
    first_row = row == 0
    on_even = place_ref[3] == 0
    for j in range(9):
        beside, beyond = beside_ref[j], beyond_ref[j]
        above = jnp.where(on_even, beyond, beside)
        below = jnp.where(on_even, beside, beyond)
        added = (
            jnp.where(first_row, above, pltpu.roll(below, 32, 1)),
            jnp.where(first_row, pltpu.roll(above, 96, 1), below),
        )
        half = place_ref[0]
        for g in range(2):
            slot = half if g == 0 else 1 - half
            tile = own_ref[j, slot] + added[g]
            if j < 8:
                out_ref[j, slot] = tile
            if j >= 7:
                history_ref[j - 7, slot] = tile


def send1_kernel(tiles_ref, history_ref, out_ref):
    for w in range(W):
        for q in range(5):
            j = 4 * w + q - 1
            tile = history_ref[0] if j < 0 else tiles_ref[j]
            if j == 0:
                tile = tile + history_ref[1]
            for x in range(X):
                out_ref[X * w + x, q] = tile


def conv2_kernel(
    place_ref, second_ref, weight_ref, partner_ref, others_ref, gain_ref, mask_ref, kept_ref,
    out_ref, high_ref, low_ref, w_high_ref, w_low_ref,
):
    lane, _, _ = lanes()
    low_half = lane < 64
    gain = column(gain_ref[...])
    half, inner = place_ref[0], place_ref[1]
    for q in range(5):
        blocks = []
        for slot in range(2):
            for u in range(W):
                source = jnp.where(half == slot, u, 1 - u)
                blocks += [second_ref[X * source + x, q, slot] for x in range(X)]
        high, low = split(norm_silu(jnp.concatenate(blocks, axis=0), gain))
        high_ref[:, 128 * q : 128 * q + 128] = high
        low_ref[:, 128 * q : 128 * q + 128] = low
    mine = 2 * half + inner
    beside = 2 * half + 1 - inner
    for slot, value in (
        (mine, weight_ref[...]),
        (3 - mine, partner_ref[...]),
        (beside, others_ref[0]),
        (3 - beside, others_ref[1]),
    ):
        w_high_ref[slot], w_low_ref[slot] = split(value)
    first = 4 * mine

    def step(g, _):
        product = dot3(w_high_ref[g], w_low_ref[g], high_ref[...], low_ref[...])
        before = taps(product[:, :128])
        for q in range(4):
            now = taps(product[:, 128 * (q + 1) : 128 * (q + 2)])
            done = in_time(
                now, before, mask_ref[0, pl.ds(first + q, 1)], mask_ref[1, pl.ds(first + q, 1)]
            )
            own = done[:16] + kept_ref[q, g]
            leave = done[16:]
            out_ref[q, g] = jnp.where(low_half, own, pltpu.roll(leave, 64, 1))
            out_ref[q + 4, g] = jnp.where(low_half, pltpu.roll(own, 64, 1), leave)
            before = now
        return 0

    lax.fori_loop(0, 4, step, 0)


def join2_kernel(parts_ref, out_ref):
    lane, _, _ = lanes()
    first_row, low_half = lane < 32, lane < 64
    zero = jnp.zeros((16, 128), f32)

    def band(s):
        above = parts_ref[s - 1] if s > 0 else zero
        below = parts_ref[s + 1] if s < SPACE - 1 else zero
        return parts_ref[s] + jnp.where(
            first_row, pltpu.roll(above, 32, 1), pltpu.roll(below, 96, 1)
        )

    for p in range(16):
        tile = jnp.where(low_half, band(2 * p), pltpu.roll(band(2 * p + 1), 64, 1))
        for i in range(X * L):
            out_ref[i, p] = tile


def attend_kernel(
    place_ref, mine_ref, other_ref, gain_ref, qk_ref, value_ref, proj_ref, out_ref,
    blocked_ref, normed_ref, high_ref, low_ref,
):
    gain = column(gain_ref[...])
    even = place_ref[3] == 0
    for p in range(16):
        mine, other = mine_ref[:, p], other_ref[:, p]
        on_0 = jnp.where(even, mine, other)
        on_1 = jnp.where(even, other, mine)
        blocks = []
        for l in range(L):
            for part in (on_0, on_1):
                blocks += [part[2 * x + l] for x in range(X)]
        tile = jnp.concatenate(blocks, axis=0)
        blocked_ref[p] = tile
        normed = tile * lax.rsqrt(jnp.mean(tile * tile, axis=0, keepdims=True) + epsilon) * gain
        normed_ref[:, 128 * p : 128 * p + 128] = normed
        high, low = split(normed)
        high_ref[:, 128 * p : 128 * p + 128] = high
        low_ref[:, 128 * p : 128 * p + 128] = low
    at = place_ref[4]
    rows = blocked_ref[at].T
    normed_rows = rows * lax.rsqrt(jnp.mean(rows * rows, axis=1, keepdims=True) + epsilon) * gain_ref[...]
    queries = jnp.dot(normed_rows, qk_ref[0], precision=highest, preferred_element_type=f32)
    queries = lax.dot_general(
        queries, qk_ref[1], (((1,), (1,)), ((), ())), precision=highest, preferred_element_type=f32
    ) * (1.0 / math.sqrt(256))
    scores = jnp.dot(queries, normed_ref[...], precision=highest, preferred_element_type=f32)
    weights = jnp.exp(scores - jnp.max(scores, axis=1, keepdims=True))
    total = jnp.sum(weights, axis=1, keepdims=True)
    e_high, e_low = split(weights)
    attended = dot3(e_high, e_low, high_ref[...], low_ref[...], ((1,), (1,))) / total
    attended = jnp.dot(attended, value_ref[...], precision=highest, preferred_element_type=f32)
    attended = jnp.dot(attended, proj_ref[...], precision=highest, preferred_element_type=f32)
    result = rows + attended
    swapped = place_ref[5]
    out_ref[swapped] = result[:64]
    out_ref[1 - swapped] = result[64:]


def delivery():
    routes = ([], [])
    for x in range(X):
        for k in range(K):
            for l in range(L):
                for c in range(CORES):
                    source = ((x * K + k) * L + l) * CORES + c
                    chip = (2 * k + l + OFFSETS[x][c]) % (K * L)
                    f = k // 4
                    for route, core in zip(routes, (f, 1 - f)):
                        route.append((source, ((k % 4) * K * L + chip) * CORES + core))
    return routes


def body(
    video,
    clip_ids,
    norm1_gain,
    conv1_weight,
    norm2_gain,
    conv2_weight,
    norm3_gain,
    qk_weight,
    value_weight,
    proj_weight,
):
    space = ("k", "l", "c")
    h, w, x, k, l, c = (lax.axis_index(n) for n in ("h", "w", "x", "k", "l", "c"))
    offset = jnp.where(c == 0, jnp.where(x == 0, 0, 2 * x), jnp.where(x == 0, 8, -2 * x))
    place = jnp.stack([h, w, x, c, (2 * k + l + offset) % (K * L), k // 4]).astype(jnp.int32)

    earlier = jnp.concatenate([jnp.full((2,), -1, jnp.int32), clip_ids])
    same = jnp.stack([earlier[1:-1] == clip_ids, earlier[:-2] == clip_ids]).astype(f32)
    masks = jnp.repeat(same, 64, axis=1).reshape(2, 16, 128)
    masks = jnp.concatenate([masks, jnp.zeros((2, 1, 128), f32)], axis=1)

    mirror = [(i, 3 - i) for i in range(H * W)]
    weight_1 = conv1_weight.reshape(432, 256)
    weight_2 = conv2_weight.reshape(432, 256)
    partner_1 = lax.ppermute(weight_1, ("h", "w"), mirror)
    partner_2 = lax.ppermute(weight_2, ("h", "w"), mirror)
    others_2 = lax.ppermute(jnp.stack([weight_2, partner_2]), "w", [(0, 1), (1, 0)])

    spread = call(spread_kernel, shape(W * X, 256, 128), [], video.reshape(128, 256))
    gathered = lax.all_to_all(spread, ("w", "x"), 0, 0)
    weights_scratch = [pltpu.VMEM((2, 432, 256), bf16)] * 2
    own, beside, beyond, kept = call(
        conv1_kernel,
        [shape(9, 2, 16, 128), shape(9, 16, 128), shape(9, 16, 128), shape(4, H * W, 16, 128)],
        weights_scratch + [pltpu.VMEM((2, 432, 256), f32)],
        place,
        gathered.reshape(W * X, H * W, X, 16, 128),
        weight_1,
        partner_1,
        norm1_gain.reshape(1, 256),
        masks,
        smem=1,
    )
    between_chips = [(i, i + 1) for i in range(1, SPACE - 1, 2)]
    beyond = lax.ppermute(beyond, space, between_chips + [(j, i) for i, j in between_chips])
    beside = lax.ppermute(beside, "c", [(0, 1), (1, 0)])
    tiles, history = call(
        join1_kernel,
        [shape(8, 2, 16, 128), shape(2, 2, 16, 128)],
        [],
        place,
        own,
        beside,
        beyond,
        smem=1,
    )
    history = lax.ppermute(history, ("h", "w"), mirror[: H * W // 2])
    second = call(send1_kernel, shape(W * X, 5, 2, 16, 128), [], tiles, history)
    second = lax.all_to_all(second, ("w", "x"), 0, 0)
    parts = call(
        conv2_kernel,
        shape(K, 4, 16, 128),
        [pltpu.VMEM((256, 640), bf16)] * 2 + [pltpu.VMEM((4, 432, 256), bf16)] * 2,
        place,
        second,
        weight_2,
        partner_2,
        others_2,
        norm2_gain.reshape(1, 256),
        masks,
        kept,
        smem=1,
    )
    parts = lax.all_to_all(parts.reshape(SPACE, 16, 128), space, 0, 0)
    frame = call(join2_kernel, shape(X * L, 16, 16, 128), [], parts)
    mine = lax.all_to_all(frame, ("x", "l"), 0, 0)
    other = lax.ppermute(mine, "c", [(0, 1), (1, 0)])
    encoded = call(
        attend_kernel,
        shape(2, 64, 256),
        [
            pltpu.VMEM((16, 256, 128), f32),
            pltpu.VMEM((256, 2048), f32),
            pltpu.VMEM((256, 2048), bf16),
            pltpu.VMEM((256, 2048), bf16),
        ],
        place,
        mine,
        other,
        norm3_gain.reshape(1, 256),
        qk_weight,
        value_weight,
        proj_weight,
        smem=1,
    )
    route_0, route_1 = delivery()
    same_core = lax.ppermute(encoded[0], ("x", "k", "l", "c"), route_0)
    other_core = lax.ppermute(encoded[1], ("x", "k", "l", "c"), route_1)
    first_frame = jnp.where(c == 0, same_core, other_core)
    second_frame = jnp.where(c == 0, other_core, same_core)
    return jnp.stack([first_frame, second_frame]).reshape(video.shape)


def solution(mesh):
    grid = Mesh(mesh.devices.reshape(H, W, X, K, L, CORES), ("h", "w", "x", "k", "l", "c"))
    tm, space = ("h", "w", "x"), ("k", "l", "c")
    in_specs = (
        P(tm, space, None, None),
        P(),
        P(),
        P(None, None, None, tm, None),
        P(),
        P(None, None, None, tm, None),
        P(),
        P(),
        P(),
        P(),
    )
    return jax.shard_map(
        body, mesh=grid, in_specs=in_specs, out_specs=P(tm, space, None, None), check_vma=False
    )
```

```python
import math

import jax
import jax.numpy as jnp
from jax import lax
from jax.experimental import pallas as pl
from jax.experimental.pallas import tpu as pltpu
from jax.sharding import Mesh
from jax.sharding import PartitionSpec as P

highest = lax.Precision.HIGHEST
epsilon = 1e-06
f32 = jnp.float32
bf16 = jnp.bfloat16

H, W, X, K, L, CORES = 2, 2, 4, 8, 2, 2
SPACE = K * L * CORES
TILES = 8

VMEM_LIMIT = 48 * 1024 * 1024


def call(kernel, out_shape, scratch, *operands, smem=0):
    return pl.pallas_call(
        kernel,
        out_shape=out_shape,
        in_specs=[pl.BlockSpec(memory_space=pltpu.SMEM)] * smem
        + [pl.BlockSpec(memory_space=pltpu.VMEM)] * (len(operands) - smem),
        out_specs=jax.tree.map(lambda _: pl.BlockSpec(memory_space=pltpu.VMEM), out_shape),
        scratch_shapes=scratch,
        compiler_params=pltpu.CompilerParams(vmem_limit_bytes=VMEM_LIMIT),
    )(*operands)


def shape(*dims):
    return jax.ShapeDtypeStruct(dims, f32)


def column(gain_row):
    return jnp.broadcast_to(gain_row, (128, gain_row.shape[1])).T


def split(value):
    high = value.astype(bf16)
    return high, (value - high.astype(f32)).astype(bf16)


def dot3(a_high, a_low, b_high, b_low, dims=((1,), (0,))):
    def one(a, b):
        return lax.dot_general(a, b, (dims, ((), ())), preferred_element_type=f32)

    return one(a_high, b_low) + one(a_low, b_high) + one(a_high, b_high)


def norm_silu(value, gain):
    scale = lax.rsqrt(jnp.mean(value * value, axis=0, keepdims=True) + epsilon)
    value = value * scale * gain
    return value / (1.0 + jnp.exp(-value))


def lanes():
    lane = lax.broadcasted_iota(jnp.int32, (16, 128), 1)
    return lane, lane % 32, (lane // 32) % 2


def taps(product):
    _, across, row = lanes()
    left, right, first_row = across >= 1, across <= 30, row == 0
    result = []
    for a in range(3):
        rows = []
        for b in range(3):
            base = (a * 9 + b * 3) * 16
            rows.append(
                product[base + 16 : base + 32]
                + jnp.where(left, pltpu.roll(product[base : base + 16], 1, 1), 0.0)
                + jnp.where(right, pltpu.roll(product[base + 32 : base + 48], 127, 1), 0.0)
            )
        stay = jnp.where(first_row, rows[0], rows[2])
        own = rows[1] + jnp.where(first_row, pltpu.roll(stay, 96, 1), pltpu.roll(stay, 32, 1))
        leave = jnp.where(first_row, rows[2], rows[0])
        result.append(jnp.concatenate([own, leave], axis=0))
    return result


def in_time(now, before, mask_1, mask_2):
    lane = lax.broadcasted_iota(jnp.int32, (32, 128), 1)
    pair = jnp.where(lane < 64, now[1], before[1])
    return now[2] + mask_1 * pltpu.roll(pair, 64, 1) + mask_2 * before[0]


def spread_kernel(video_ref, out_ref):
    flipped = video_ref[...].T
    for i in range(W * X):
        out_ref[i] = flipped


def conv1_kernel(
    place_ref, video_ref, weight_ref, partner_ref, gain_ref, mask_ref,
    own_ref, beside_ref, beyond_ref, kept_ref, high_ref, low_ref, product_ref,
):
    _, _, row = lanes()
    first_row = row == 0
    gain = column(gain_ref[0:1])
    for g, ref in enumerate((weight_ref, partner_ref)):
        high_ref[g], low_ref[g] = split(ref[...])
    half, across, core = place_ref[0], place_ref[2], place_ref[3]
    mine = 2 * half + place_ref[1]
    for j in range(TILES):
        kept_ref[j, half] = video_ref[j, mine, across]
        kept_ref[j, 1 - half] = video_ref[j, 3 - mine, across]

    def finish(j, now, before):
        masks = mask_ref[0, pl.ds(8 * half + j, 1)], mask_ref[1, pl.ds(8 * half + j, 1)]
        outside = []
        for g in range(2):
            done = in_time(now[g], before[g], *masks)
            own_ref[j, half if g == 0 else 1 - half] = done[:16]
            outside.append(done[16:])
        up = jnp.where(first_row, outside[0], pltpu.roll(outside[1], 32, 1))
        down = jnp.where(first_row, pltpu.roll(outside[0], 96, 1), outside[1])
        on_even = core == 0
        beside_ref[j] = jnp.where(on_even, down, up)
        beyond_ref[j] = jnp.where(on_even, up, down)

    def step(p, before):
        pieces = []
        for side in range(2):
            tile = video_ref[2 * p + side].reshape(256, 128)
            pieces.append(split(norm_silu(tile, gain)))
        high = jnp.concatenate([pieces[0][0], pieces[1][0]], axis=1)
        low = jnp.concatenate([pieces[0][1], pieces[1][1]], axis=1)
        for g in range(2):
            product_ref[g] = dot3(high_ref[g], low_ref[g], high, low)
        for side in range(2):
            now = [taps(product_ref[g, :, 128 * side : 128 * side + 128]) for g in range(2)]
            finish(2 * p + side, now, before)
            before = now
        return before

    zeros = [[jnp.zeros((32, 128), f32)] * 3] * 2
    last = lax.fori_loop(0, 4, step, zeros)
    finish(8, zeros, last)


def join1_kernel(place_ref, own_ref, beside_ref, beyond_ref, out_ref, history_ref):
    _, _, row = lanes()
    first_row = row == 0
    on_even = place_ref[3] == 0
    for j in range(9):
        beside, beyond = beside_ref[j], beyond_ref[j]
        above = jnp.where(on_even, beyond, beside)
        below = jnp.where(on_even, beside, beyond)
        added = (
            jnp.where(first_row, above, pltpu.roll(below, 32, 1)),
            jnp.where(first_row, pltpu.roll(above, 96, 1), below),
        )
        half = place_ref[0]
        for g in range(2):
            slot = half if g == 0 else 1 - half
            tile = own_ref[j, slot] + added[g]
            if j < 8:
                out_ref[j, slot] = tile
            if j >= 7:
                history_ref[j - 7, slot] = tile


def send1_kernel(tiles_ref, history_ref, out_ref):
    for q in range(TILES + 1):
        tile = history_ref[0] if q == 0 else tiles_ref[q - 1]
        if q == 1:
            tile = tile + history_ref[1]
        for i in range(W * X):
            out_ref[i, q] = tile


def conv2_kernel(
    place_ref, second_ref, weight_ref, partner_ref, gain_ref, mask_ref, kept_ref,
    out_ref, high_ref, low_ref, product_ref,
):
    lane, _, _ = lanes()
    low_half = lane < 64
    gain = column(gain_ref[1:2])
    half = place_ref[0]
    for q in range(TILES + 1):
        blocks = []
        for slot in range(2):
            for u in range(W):
                source = jnp.where(half == slot, u, 1 - u)
                blocks += [second_ref[X * source + x, q, slot] for x in range(X)]
        high, low = split(norm_silu(jnp.concatenate(blocks, axis=0), gain))
        high_ref[:, 128 * q : 128 * q + 128] = high
        low_ref[:, 128 * q : 128 * q + 128] = low
    for g, ref in enumerate((weight_ref, partner_ref)):
        slot = half if g == 0 else 1 - half
        w_high, w_low = split(ref[...])
        product_ref[...] = dot3(w_high, w_low, high_ref[...], low_ref[...])
        before = taps(product_ref[:, :128])
        for q in range(TILES):
            now = taps(product_ref[:, 128 * (q + 1) : 128 * (q + 2)])
            at = TILES * half + q
            done = in_time(now, before, mask_ref[0, pl.ds(at, 1)], mask_ref[1, pl.ds(at, 1)])
            own = done[:16] + kept_ref[q, slot]
            leave = done[16:]
            out_ref[q, slot] = jnp.where(low_half, own, pltpu.roll(leave, 64, 1))
            out_ref[q + TILES, slot] = jnp.where(low_half, pltpu.roll(own, 64, 1), leave)
            before = now


def join2_kernel(parts_ref, out_ref):
    lane, _, _ = lanes()
    first_row, low_half = lane < 32, lane < 64
    zero = jnp.zeros((16, 128), f32)

    def band(s):
        above = parts_ref[s - 1] if s > 0 else zero
        below = parts_ref[s + 1] if s < SPACE - 1 else zero
        return parts_ref[s] + jnp.where(
            first_row, pltpu.roll(above, 32, 1), pltpu.roll(below, 96, 1)
        )

    for p in range(16):
        tile = jnp.where(low_half, band(2 * p), pltpu.roll(band(2 * p + 1), 64, 1))
        for i in range(W * X):
            out_ref[i, p] = tile


def attend_kernel(
    place_ref, mine_ref, other_ref, gain_ref, qk_ref, value_ref, proj_ref, out_ref,
    blocked_ref, normed_ref, high_ref, low_ref,
):
    gain = column(gain_ref[2:3])
    half, core = place_ref[0], place_ref[3]
    for p in range(16):
        blocks = []
        for slot in range(2):
            for u in range(W):
                source = X * jnp.where(half == slot, u, 1 - u)
                for x in range(X):
                    mine, other = mine_ref[source + x, p], other_ref[source + x, p]
                    blocks.append(jnp.where(core == slot, mine, other))
        tile = jnp.concatenate(blocks, axis=0)
        blocked_ref[p] = tile
        normed = tile * lax.rsqrt(jnp.mean(tile * tile, axis=0, keepdims=True) + epsilon) * gain
        normed_ref[:, 128 * p : 128 * p + 128] = normed
        high, low = split(normed)
        high_ref[:, 128 * p : 128 * p + 128] = high
        low_ref[:, 128 * p : 128 * p + 128] = low
    at = place_ref[4]
    rows = blocked_ref[at].T
    normed_rows = rows * lax.rsqrt(jnp.mean(rows * rows, axis=1, keepdims=True) + epsilon) * gain_ref[2:3]
    queries = jnp.dot(normed_rows, qk_ref[0], precision=highest, preferred_element_type=f32)
    queries = lax.dot_general(
        queries, qk_ref[1], (((1,), (1,)), ((), ())), precision=highest, preferred_element_type=f32
    ) * (1.0 / math.sqrt(256))
    scores = jnp.dot(queries, normed_ref[...], precision=highest, preferred_element_type=f32)
    weights = jnp.exp(scores - jnp.max(scores, axis=1, keepdims=True))
    total = jnp.sum(weights, axis=1, keepdims=True)
    e_high, e_low = split(weights)
    attended = dot3(e_high, e_low, high_ref[...], low_ref[...], ((1,), (1,))) / total
    attended = jnp.dot(attended, value_ref[...], precision=highest, preferred_element_type=f32)
    attended = jnp.dot(attended, proj_ref[...], precision=highest, preferred_element_type=f32)
    result = rows + attended
    swapped = place_ref[5]
    out_ref[swapped] = result[:64]
    out_ref[1 - swapped] = result[64:]


def delivery():
    routes = ([], [])
    for i in range(W * X):
        for z in range(K * L):
            for c in range(CORES):
                source = (i * K * L + z) * CORES + c
                chip = (z + (i if c == 0 else -i if i else 8)) % (K * L)
                f = z // TILES
                for route, core in zip(routes, (f, 1 - f)):
                    route.append((source, ((z % TILES) * K * L + chip) * CORES + core))
    return routes


def body(
    video,
    clip_ids,
    norm1_gain,
    conv1_weight,
    norm2_gain,
    conv2_weight,
    norm3_gain,
    qk_weight,
    value_weight,
    proj_weight,
):
    space = ("k", "l", "c")
    h, w, x, k, l, c = (lax.axis_index(n) for n in ("h", "w", "x", "k", "l", "c"))
    z, i = 2 * k + l, X * w + x
    offset = jnp.where(c == 0, i, jnp.where(i == 0, 8, K * L - i))
    place = jnp.stack([h, w, x, c, (z + offset) % (K * L), z // TILES]).astype(jnp.int32)

    earlier = jnp.concatenate([jnp.full((2,), -1, jnp.int32), clip_ids])
    same = jnp.stack([earlier[1:-1] == clip_ids, earlier[:-2] == clip_ids]).astype(f32)
    masks = jnp.repeat(same, 64, axis=1).reshape(2, 16, 128)
    masks = jnp.concatenate([masks, jnp.zeros((2, 1, 128), f32)], axis=1)

    mirror = [(i, 3 - i) for i in range(H * W)]
    weight_1 = conv1_weight.reshape(432, 256)
    weight_2 = conv2_weight.reshape(432, 256)
    partner_1 = lax.ppermute(weight_1, ("h", "w"), mirror)
    partner_2 = lax.ppermute(weight_2, ("h", "w"), mirror)
    swap = [(0, 1), (1, 0)]
    gains = jnp.stack([norm1_gain, norm2_gain, norm3_gain])

    spread = call(spread_kernel, shape(W * X, 256, 128), [], video.reshape(128, 256))
    gathered = lax.all_to_all(spread, ("w", "x"), 0, 0)
    weights_scratch = [pltpu.VMEM((2, 432, 256), bf16)] * 2
    own, beside, beyond, kept = call(
        conv1_kernel,
        [shape(9, 2, 16, 128), shape(9, 16, 128), shape(9, 16, 128), shape(TILES, 2, 16, 128)],
        weights_scratch + [pltpu.VMEM((2, 432, 256), f32)],
        place,
        gathered.reshape(W * X, H * W, X, 16, 128),
        weight_1,
        partner_1,
        gains,
        masks,
        smem=1,
    )
    between_chips = [(i, i + 1) for i in range(1, SPACE - 1, 2)]
    beyond = lax.ppermute(beyond, space, between_chips + [(j, i) for i, j in between_chips])
    beside = lax.ppermute(beside, "c", swap)
    tiles, history = call(
        join1_kernel,
        [shape(8, 2, 16, 128), shape(2, 2, 16, 128)],
        [],
        place,
        own,
        beside,
        beyond,
        smem=1,
    )
    history = lax.ppermute(history, ("h", "w"), mirror[: H * W // 2])
    second = call(send1_kernel, shape(W * X, TILES + 1, 2, 16, 128), [], tiles, history)
    second = lax.all_to_all(second, ("w", "x"), 0, 0)
    parts = call(
        conv2_kernel,
        shape(K * L, CORES, 16, 128),
        [pltpu.VMEM((256, 1152), bf16)] * 2 + [pltpu.VMEM((432, 1152), f32)],
        place,
        second,
        weight_2,
        partner_2,
        gains,
        masks,
        kept,
        smem=1,
    )
    parts = lax.all_to_all(parts.reshape(SPACE, 16, 128), space, 0, 0)
    frame = call(join2_kernel, shape(W * X, 16, 16, 128), [], parts)
    mine = lax.all_to_all(frame, ("w", "x"), 0, 0)
    other = lax.ppermute(mine, "c", swap)
    encoded = call(
        attend_kernel,
        shape(2, 64, 256),
        [
            pltpu.VMEM((16, 256, 128), f32),
            pltpu.VMEM((256, 2048), f32),
            pltpu.VMEM((256, 2048), bf16),
            pltpu.VMEM((256, 2048), bf16),
        ],
        place,
        mine,
        other,
        gains,
        qk_weight,
        value_weight,
        proj_weight,
        smem=1,
    )
    route_0, route_1 = delivery()
    same_core = lax.ppermute(encoded[0], ("w", "x", "k", "l", "c"), route_0)
    other_core = lax.ppermute(encoded[1], ("w", "x", "k", "l", "c"), route_1)
    first_frame = jnp.where(c == 0, same_core, other_core)
    second_frame = jnp.where(c == 0, other_core, same_core)
    return jnp.stack([first_frame, second_frame]).reshape(video.shape)


def solution(mesh):
    grid = Mesh(mesh.devices.reshape(H, W, X, K, L, CORES), ("h", "w", "x", "k", "l", "c"))
    tm, space = ("h", "w", "x"), ("k", "l", "c")
    in_specs = (
        P(tm, space, None, None),
        P(),
        P(),
        P(None, None, None, tm, None),
        P(),
        P(None, None, None, tm, None),
        P(),
        P(),
        P(),
        P(),
    )
    return jax.shard_map(
        body, mesh=grid, in_specs=in_specs, out_specs=P(tm, space, None, None), check_vma=False
    )
```

```python
import math

import jax
import jax.numpy as jnp
from jax import lax
from jax.experimental import pallas as pl
from jax.experimental.pallas import tpu as pltpu
from jax.sharding import Mesh
from jax.sharding import PartitionSpec as P

highest = lax.Precision.HIGHEST
epsilon = 1e-06
f32 = jnp.float32
bf16 = jnp.bfloat16

H, W, X, K, L, CORES = 2, 2, 4, 8, 2, 2
SPACE = K * L * CORES
TILES = 8

VMEM_LIMIT = 48 * 1024 * 1024


def call(kernel, out_shape, scratch, *operands, smem=0):
    return pl.pallas_call(
        kernel,
        out_shape=out_shape,
        in_specs=[pl.BlockSpec(memory_space=pltpu.SMEM)] * smem
        + [pl.BlockSpec(memory_space=pltpu.VMEM)] * (len(operands) - smem),
        out_specs=jax.tree.map(lambda _: pl.BlockSpec(memory_space=pltpu.VMEM), out_shape),
        scratch_shapes=scratch,
        compiler_params=pltpu.CompilerParams(vmem_limit_bytes=VMEM_LIMIT),
    )(*operands)


def shape(*dims):
    return jax.ShapeDtypeStruct(dims, f32)


def column(gain_row):
    return jnp.broadcast_to(gain_row, (128, gain_row.shape[1])).T


def split(value):
    high = value.astype(bf16)
    return high, (value - high.astype(f32)).astype(bf16)


def dot3(a_high, a_low, b_high, b_low, dims=((1,), (0,))):
    def one(a, b):
        return lax.dot_general(a, b, (dims, ((), ())), preferred_element_type=f32)

    return one(a_high, b_low) + one(a_low, b_high) + one(a_high, b_high)


def norm_silu(value, gain):
    scale = lax.rsqrt(jnp.mean(value * value, axis=0, keepdims=True) + epsilon)
    value = value * scale * gain
    return value / (1.0 + jnp.exp(-value))


def lanes():
    lane = lax.broadcasted_iota(jnp.int32, (16, 128), 1)
    return lane, lane % 32, (lane // 32) % 2


def taps(product):
    _, across, row = lanes()
    left, right, first_row = across >= 1, across <= 30, row == 0
    result = []
    for a in range(3):
        rows = []
        for b in range(3):
            base = (a * 9 + b * 3) * 16
            rows.append(
                product[base + 16 : base + 32]
                + jnp.where(left, pltpu.roll(product[base : base + 16], 1, 1), 0.0)
                + jnp.where(right, pltpu.roll(product[base + 32 : base + 48], 127, 1), 0.0)
            )
        stay = jnp.where(first_row, rows[0], rows[2])
        own = rows[1] + jnp.where(first_row, pltpu.roll(stay, 96, 1), pltpu.roll(stay, 32, 1))
        leave = jnp.where(first_row, rows[2], rows[0])
        result.append(jnp.concatenate([own, leave], axis=0))
    return result


def in_time(now, before, mask_1, mask_2):
    lane = lax.broadcasted_iota(jnp.int32, (32, 128), 1)
    pair = jnp.where(lane < 64, now[1], before[1])
    return now[2] + mask_1 * pltpu.roll(pair, 64, 1) + mask_2 * before[0]


def spread_kernel(video_ref, out_ref):
    flipped = video_ref[...].T
    for i in range(W * X):
        out_ref[i] = flipped


def conv1_kernel(
    place_ref, video_ref, weight_ref, partner_ref, gain_ref, mask_ref,
    own_ref, beside_ref, beyond_ref, kept_ref, high_ref, low_ref, product_ref,
):
    _, _, row = lanes()
    first_row = row == 0
    gain = column(gain_ref[0:1])
    for g, ref in enumerate((weight_ref, partner_ref)):
        high_ref[g], low_ref[g] = split(ref[...])
    half, across, core = place_ref[0], place_ref[2], place_ref[3]
    mine = 2 * half + place_ref[1]
    for j in range(TILES):
        kept_ref[j, half] = video_ref[j, mine, across]
        kept_ref[j, 1 - half] = video_ref[j, 3 - mine, across]

    def finish(j, now, before):
        masks = mask_ref[0, pl.ds(8 * half + j, 1)], mask_ref[1, pl.ds(8 * half + j, 1)]
        outside = []
        for g in range(2):
            done = in_time(now[g], before[g], *masks)
            own_ref[j, half if g == 0 else 1 - half] = done[:16]
            outside.append(done[16:])
        up = jnp.where(first_row, outside[0], pltpu.roll(outside[1], 32, 1))
        down = jnp.where(first_row, pltpu.roll(outside[0], 96, 1), outside[1])
        on_even = core == 0
        beside_ref[j] = jnp.where(on_even, down, up)
        beyond_ref[j] = jnp.where(on_even, up, down)

    def step(p, before):
        pieces = []
        for side in range(2):
            tile = video_ref[2 * p + side].reshape(256, 128)
            pieces.append(split(norm_silu(tile, gain)))
        high = jnp.concatenate([pieces[0][0], pieces[1][0]], axis=1)
        low = jnp.concatenate([pieces[0][1], pieces[1][1]], axis=1)
        for g in range(2):
            product_ref[g] = dot3(high_ref[g], low_ref[g], high, low)
        for side in range(2):
            now = [taps(product_ref[g, :, 128 * side : 128 * side + 128]) for g in range(2)]
            finish(2 * p + side, now, before)
            before = now
        return before

    zeros = [[jnp.zeros((32, 128), f32)] * 3] * 2
    last = zeros
    for p in range(TILES // 2):
        last = step(p, last)
    finish(TILES, zeros, last)


def join1_kernel(place_ref, own_ref, beside_ref, beyond_ref, out_ref, history_ref):
    _, _, row = lanes()
    first_row = row == 0
    on_even = place_ref[3] == 0
    for j in range(9):
        beside, beyond = beside_ref[j], beyond_ref[j]
        above = jnp.where(on_even, beyond, beside)
        below = jnp.where(on_even, beside, beyond)
        added = (
            jnp.where(first_row, above, pltpu.roll(below, 32, 1)),
            jnp.where(first_row, pltpu.roll(above, 96, 1), below),
        )
        half = place_ref[0]
        for g in range(2):
            slot = half if g == 0 else 1 - half
            tile = own_ref[j, slot] + added[g]
            if j < 8:
                out_ref[j, slot] = tile
            if j >= 7:
                history_ref[j - 7, slot] = tile


def send1_kernel(tiles_ref, history_ref, out_ref):
    for q in range(TILES + 1):
        tile = history_ref[0] if q == 0 else tiles_ref[q - 1]
        if q == 1:
            tile = tile + history_ref[1]
        for i in range(W * X):
            out_ref[i, q] = tile


def conv2_kernel(
    place_ref, second_ref, weight_ref, partner_ref, gain_ref, mask_ref, kept_ref,
    out_ref, high_ref, low_ref, product_ref,
):
    lane, _, _ = lanes()
    low_half = lane < 64
    gain = column(gain_ref[1:2])
    half = place_ref[0]
    for q in range(TILES + 1):
        blocks = []
        for slot in range(2):
            for u in range(W):
                source = jnp.where(half == slot, u, 1 - u)
                blocks += [second_ref[X * source + x, q, slot] for x in range(X)]
        high, low = split(norm_silu(jnp.concatenate(blocks, axis=0), gain))
        high_ref[:, 128 * q : 128 * q + 128] = high
        low_ref[:, 128 * q : 128 * q + 128] = low
    for g, ref in enumerate((weight_ref, partner_ref)):
        slot = half if g == 0 else 1 - half
        w_high, w_low = split(ref[...])
        product_ref[...] = dot3(w_high, w_low, high_ref[...], low_ref[...])
        before = taps(product_ref[:, :128])
        for q in range(TILES):
            now = taps(product_ref[:, 128 * (q + 1) : 128 * (q + 2)])
            at = TILES * half + q
            done = in_time(now, before, mask_ref[0, pl.ds(at, 1)], mask_ref[1, pl.ds(at, 1)])
            own = done[:16] + kept_ref[q, slot]
            leave = done[16:]
            out_ref[q, slot] = jnp.where(low_half, own, pltpu.roll(leave, 64, 1))
            out_ref[q + TILES, slot] = jnp.where(low_half, pltpu.roll(own, 64, 1), leave)
            before = now


def join2_kernel(parts_ref, out_ref):
    lane, _, _ = lanes()
    first_row, low_half = lane < 32, lane < 64
    zero = jnp.zeros((16, 128), f32)

    def band(s):
        above = parts_ref[s - 1] if s > 0 else zero
        below = parts_ref[s + 1] if s < SPACE - 1 else zero
        return parts_ref[s] + jnp.where(
            first_row, pltpu.roll(above, 32, 1), pltpu.roll(below, 96, 1)
        )

    for p in range(16):
        tile = jnp.where(low_half, band(2 * p), pltpu.roll(band(2 * p + 1), 64, 1))
        for i in range(W * X):
            out_ref[i, p] = tile


def fold_kernel(qk_ref, value_ref, proj_ref, out_ref):
    scores = lax.dot_general(
        qk_ref[0], qk_ref[1], (((1,), (1,)), ((), ())), precision=highest, preferred_element_type=f32
    )
    out_ref[0] = scores * (1.0 / math.sqrt(256))
    out_ref[1] = jnp.dot(
        value_ref[...], proj_ref[...], precision=highest, preferred_element_type=f32
    )


def attend_kernel(
    place_ref, mine_ref, other_ref, gain_ref, folded_ref, same_ref, cross_ref,
    blocked_ref, high_ref, low_ref,
):
    gain = column(gain_ref[2:3])
    half, core = place_ref[0], place_ref[3]
    for p in range(16):
        blocks = []
        for slot in range(2):
            for u in range(W):
                source = X * jnp.where(half == slot, u, 1 - u)
                for x in range(X):
                    mine, other = mine_ref[source + x, p], other_ref[source + x, p]
                    blocks.append(jnp.where(core == slot, mine, other))
        tile = jnp.concatenate(blocks, axis=0)
        blocked_ref[p] = tile
        normed = tile * lax.rsqrt(jnp.mean(tile * tile, axis=0, keepdims=True) + epsilon) * gain
        high, low = split(normed)
        high_ref[:, 128 * p : 128 * p + 128] = high
        low_ref[:, 128 * p : 128 * p + 128] = low
    at = place_ref[4]
    rows = blocked_ref[at].T
    normed = rows * lax.rsqrt(jnp.mean(rows * rows, axis=1, keepdims=True) + epsilon) * gain_ref[2:3]
    queries = dot3(*split(normed), *split(folded_ref[0]))
    scores = dot3(*split(queries), high_ref[...], low_ref[...])
    weights = jnp.exp(scores - jnp.max(scores, axis=1, keepdims=True))
    total = jnp.sum(weights, axis=1, keepdims=True)
    attended = dot3(*split(weights), high_ref[...], low_ref[...], ((1,), (1,))) / total
    result = rows + dot3(*split(attended), *split(folded_ref[1]))
    first_core = place_ref[5] == 0
    same_ref[...] = jnp.where(first_core, result[:64], result[64:])
    cross_ref[...] = jnp.where(first_core, result[64:], result[:64])


def delivery():
    routes = ([], [])
    for i in range(W * X):
        for z in range(K * L):
            for c in range(CORES):
                source = (i * K * L + z) * CORES + c
                chip = (z + (i if c == 0 else -i if i else 8)) % (K * L)
                f = z // TILES
                for route, core in zip(routes, (f, 1 - f)):
                    route.append((source, ((z % TILES) * K * L + chip) * CORES + core))
    return routes


def body(
    video,
    clip_ids,
    norm1_gain,
    conv1_weight,
    norm2_gain,
    conv2_weight,
    norm3_gain,
    qk_weight,
    value_weight,
    proj_weight,
):
    space = ("k", "l", "c")
    h, w, x, k, l, c = (lax.axis_index(n) for n in ("h", "w", "x", "k", "l", "c"))
    z, i = 2 * k + l, X * w + x
    offset = jnp.where(c == 0, i, jnp.where(i == 0, 8, K * L - i))
    place = jnp.stack([h, w, x, c, (z + offset) % (K * L), z // TILES]).astype(jnp.int32)

    earlier = jnp.concatenate([jnp.full((2,), -1, jnp.int32), clip_ids])
    same = jnp.stack([earlier[1:-1] == clip_ids, earlier[:-2] == clip_ids]).astype(f32)
    masks = jnp.repeat(same, 64, axis=1).reshape(2, 16, 128)
    masks = jnp.concatenate([masks, jnp.zeros((2, 1, 128), f32)], axis=1)

    mirror = [(i, 3 - i) for i in range(H * W)]
    weight_1 = conv1_weight.reshape(432, 256)
    weight_2 = conv2_weight.reshape(432, 256)
    partner_1 = lax.ppermute(weight_1, ("h", "w"), mirror)
    partner_2 = lax.ppermute(weight_2, ("h", "w"), mirror)
    swap = [(0, 1), (1, 0)]
    gains = jnp.stack([norm1_gain, norm2_gain, norm3_gain])

    folded = call(fold_kernel, shape(2, 256, 256), [], qk_weight, value_weight, proj_weight)
    spread = call(spread_kernel, shape(W * X, 256, 128), [], video.reshape(128, 256))
    gathered = lax.all_to_all(spread, ("w", "x"), 0, 0)
    weights_scratch = [pltpu.VMEM((2, 432, 256), bf16)] * 2
    own, beside, beyond, kept = call(
        conv1_kernel,
        [shape(9, 2, 16, 128), shape(9, 16, 128), shape(9, 16, 128), shape(TILES, 2, 16, 128)],
        weights_scratch + [pltpu.VMEM((2, 432, 256), f32)],
        place,
        gathered.reshape(W * X, H * W, X, 16, 128),
        weight_1,
        partner_1,
        gains,
        masks,
        smem=1,
    )
    between_chips = [(i, i + 1) for i in range(1, SPACE - 1, 2)]
    beyond = lax.ppermute(beyond, space, between_chips + [(j, i) for i, j in between_chips])
    beside = lax.ppermute(beside, "c", swap)
    tiles, history = call(
        join1_kernel,
        [shape(8, 2, 16, 128), shape(2, 2, 16, 128)],
        [],
        place,
        own,
        beside,
        beyond,
        smem=1,
    )
    history = lax.ppermute(history, ("h", "w"), mirror[: H * W // 2])
    second = call(send1_kernel, shape(W * X, TILES + 1, 2, 16, 128), [], tiles, history)
    second = lax.all_to_all(second, ("w", "x"), 0, 0)
    parts = call(
        conv2_kernel,
        shape(K * L, CORES, 16, 128),
        [pltpu.VMEM((256, 1152), bf16)] * 2 + [pltpu.VMEM((432, 1152), f32)],
        place,
        second,
        weight_2,
        partner_2,
        gains,
        masks,
        kept,
        smem=1,
    )
    parts = lax.all_to_all(parts.reshape(SPACE, 16, 128), space, 0, 0)
    frame = call(join2_kernel, shape(W * X, 16, 16, 128), [], parts)
    mine = lax.all_to_all(frame, ("w", "x"), 0, 0)
    other = lax.ppermute(mine, "c", swap)
    same_core, other_core = call(
        attend_kernel,
        [shape(64, 256), shape(64, 256)],
        [
            pltpu.VMEM((16, 256, 128), f32),
            pltpu.VMEM((256, 2048), bf16),
            pltpu.VMEM((256, 2048), bf16),
        ],
        place,
        mine,
        other,
        gains,
        folded,
        smem=1,
    )
    route_0, route_1 = delivery()
    same_core = lax.ppermute(same_core, ("w", "x", "k", "l", "c"), route_0)
    other_core = lax.ppermute(other_core, ("w", "x", "k", "l", "c"), route_1)
    first_frame = jnp.where(c == 0, same_core, other_core)
    second_frame = jnp.where(c == 0, other_core, same_core)
    return jnp.stack([first_frame, second_frame]).reshape(video.shape)


def solution(mesh):
    grid = Mesh(mesh.devices.reshape(H, W, X, K, L, CORES), ("h", "w", "x", "k", "l", "c"))
    tm, space = ("h", "w", "x"), ("k", "l", "c")
    in_specs = (
        P(tm, space, None, None),
        P(),
        P(),
        P(None, None, None, tm, None),
        P(),
        P(None, None, None, tm, None),
        P(),
        P(),
        P(),
        P(),
    )
    return jax.shard_map(
        body, mesh=grid, in_specs=in_specs, out_specs=P(tm, space, None, None), check_vma=False
    )
```

```python
import math

import jax
import jax.numpy as jnp
import numpy as np
from jax import lax
from jax.experimental import pallas as pl
from jax.experimental.pallas import tpu as pltpu
from jax.sharding import Mesh
from jax.sharding import PartitionSpec as P

highest = lax.Precision.HIGHEST
epsilon = 1e-06
f32 = jnp.float32
bf16 = jnp.bfloat16

H, W, X, K, L, CORES = 2, 2, 4, 8, 2, 2
SPACE = K * L * CORES
TILES = 8

VMEM_LIMIT = 48 * 1024 * 1024


def call(kernel, out_shape, scratch, *operands, smem=0):
    return pl.pallas_call(
        kernel,
        out_shape=out_shape,
        in_specs=[pl.BlockSpec(memory_space=pltpu.SMEM)] * smem
        + [pl.BlockSpec(memory_space=pltpu.VMEM)] * (len(operands) - smem),
        out_specs=jax.tree.map(lambda _: pl.BlockSpec(memory_space=pltpu.VMEM), out_shape),
        scratch_shapes=scratch,
        compiler_params=pltpu.CompilerParams(vmem_limit_bytes=VMEM_LIMIT),
    )(*operands)


def shape(*dims):
    return jax.ShapeDtypeStruct(dims, f32)


def column(gain_row):
    return jnp.broadcast_to(gain_row, (128, gain_row.shape[1])).T


def split(value):
    high = value.astype(bf16)
    return high, (value - high.astype(f32)).astype(bf16)


def dot3(a_high, a_low, b_high, b_low, dims=((1,), (0,))):
    def one(a, b):
        return lax.dot_general(a, b, (dims, ((), ())), preferred_element_type=f32)

    return one(a_high, b_low) + one(a_low, b_high) + one(a_high, b_high)


def dot3_stacked(a_high, a_low, b_high, b_low, dims=((1,), (0,))):
    def one(a, b):
        return lax.dot_general(a, b, (dims, ((), ())), preferred_element_type=f32)

    rows = a_high.shape[0]
    both = one(jnp.concatenate([a_high, a_low], axis=0), b_high)
    return both[:rows] + (both[rows:] + one(a_high, b_low))


def norm_silu(value, gain):
    scale = lax.rsqrt(jnp.mean(value * value, axis=0, keepdims=True) + epsilon)
    value = value * scale * gain
    return value / (1.0 + jnp.exp(-value))


def lanes():
    lane = lax.broadcasted_iota(jnp.int32, (16, 128), 1)
    return lane, lane % 32, (lane // 32) % 2


def row_taps(product, a):
    _, across, _ = lanes()
    left, right = across >= 1, across <= 30
    rows = []
    for b in range(3):
        base = (a * 9 + b * 3) * 16
        rows.append(
            product[base + 16 : base + 32]
            + jnp.where(left, pltpu.roll(product[base : base + 16], 1, 1), 0.0)
            + jnp.where(right, pltpu.roll(product[base + 32 : base + 48], 127, 1), 0.0)
        )
    return rows


def taps_shifted(product):
    _, _, row = lanes()
    first_row = row == 0
    result = []
    for a in range(3):
        rows = row_taps(product, a)
        stay = rows[2] + jnp.where(first_row, 0.0, pltpu.roll(rows[1], 32, 1))
        go = rows[0] + jnp.where(first_row, pltpu.roll(rows[1], 96, 1), 0.0)
        result.append(jnp.concatenate([stay, go], axis=0))
    return result


def taps(product, adjacent):
    _, _, row = lanes()
    first_row = row == 0
    result = []
    for a in range(3):
        rows = row_taps(product, a)
        cross = jnp.where(first_row, rows[0], rows[2])
        cross = jnp.where(first_row, pltpu.roll(cross, 96, 1), pltpu.roll(cross, 32, 1))
        own = rows[1] + jnp.where(adjacent, cross, 0.0)
        leave = jnp.where(first_row, rows[2], rows[0])
        result.append(jnp.concatenate([own, leave], axis=0))
    return result


def in_time(now, before, mask_1, mask_2):
    lane = lax.broadcasted_iota(jnp.int32, (32, 128), 1)
    pair = jnp.where(lane < 64, now[1], before[1])
    return now[2] + mask_1 * pltpu.roll(pair, 64, 1) + mask_2 * before[0]


def spread_kernel(video_ref, out_ref):
    flipped = video_ref[...].T
    for i in range(W * X):
        out_ref[i] = flipped


def conv1_kernel(
    place_ref, video_ref, weight_ref, partner_ref, gain_ref, mask_ref,
    own_ref, onward_ref, kept_ref, high_ref, low_ref, product_ref,
):
    gain = column(gain_ref[0:1])
    for g, ref in enumerate((weight_ref, partner_ref)):
        high_ref[g], low_ref[g] = split(ref[...])
    half, across = place_ref[0], place_ref[2]
    mine = 2 * half + place_ref[1]

    def finish(j, now, before):
        masks = mask_ref[0, pl.ds(8 * half + j, 1)], mask_ref[1, pl.ds(8 * half + j, 1)]
        for g in range(2):
            slot = half if g == 0 else 1 - half
            done = in_time(now[g], before[g], *masks)
            own_ref[j, slot] = done[:16]
            onward_ref[j, slot] = done[16:]

    def step(p, before):
        pieces = []
        for side in range(2):
            j = 2 * p + side
            kept_ref[j, half] = video_ref[j, mine, across]
            kept_ref[j, 1 - half] = video_ref[j, 3 - mine, across]
            tile = video_ref[j].reshape(256, 128)
            pieces.append(split(norm_silu(tile, gain)))
        high = jnp.concatenate([pieces[0][0], pieces[1][0]], axis=1)
        low = jnp.concatenate([pieces[0][1], pieces[1][1]], axis=1)
        for g in range(2):
            product_ref[g] = dot3(high_ref[g], low_ref[g], high, low)
        for side in range(2):
            now = [taps_shifted(product_ref[g, :, 128 * side : 128 * side + 128]) for g in range(2)]
            finish(2 * p + side, now, before)
            before = now
        return before

    zeros = [[jnp.zeros((32, 128), f32)] * 3] * 2
    last = zeros
    for p in range(TILES // 2):
        last = step(p, last)
    finish(TILES, zeros, last)


def join1_kernel(place_ref, own_ref, arrived_ref, out_ref, history_ref):
    _, _, row = lanes()
    first_row = row == 0
    at_edge = place_ref[6] == 0
    for j in range(TILES + 1):
        for slot in range(2):
            own, arrived = own_ref[j, slot], arrived_ref[j, slot]
            edge = jnp.where(first_row, arrived, own)
            tile = jnp.where(at_edge, edge, own + arrived)
            if j < TILES:
                out_ref[j, slot] = tile
            if j >= TILES - 1:
                history_ref[j - TILES + 1, slot] = tile


def send1_kernel(tiles_ref, history_ref, out_ref):
    for q in range(TILES + 1):
        tile = history_ref[0] if q == 0 else tiles_ref[q - 1]
        if q == 1:
            tile = tile + history_ref[1]
        for i in range(W * X):
            out_ref[i, q] = tile


def conv2_kernel(
    place_ref, second_ref, weight_ref, partner_ref, gain_ref, mask_ref, kept_ref,
    out_ref, high_ref, low_ref, product_ref,
):
    lane, _, row = lanes()
    low_half, second_row = lane < 64, row == 1
    adjacent = place_ref[6] != 0
    gain = column(gain_ref[1:2])
    half = place_ref[0]
    for q in range(TILES + 1):
        blocks = []
        for slot in range(2):
            for u in range(W):
                source = jnp.where(half == slot, u, 1 - u)
                blocks += [second_ref[X * source + x, q, slot] for x in range(X)]
        high, low = split(norm_silu(jnp.concatenate(blocks, axis=0), gain))
        high_ref[:, 128 * q : 128 * q + 128] = high
        low_ref[:, 128 * q : 128 * q + 128] = low
    for g, ref in enumerate((weight_ref, partner_ref)):
        slot = half if g == 0 else 1 - half
        w_high, w_low = split(ref[...])
        product_ref[...] = dot3(w_high, w_low, high_ref[...], low_ref[...])
        before = taps(product_ref[:, :128], adjacent)
        for q in range(TILES):
            now = taps(product_ref[:, 128 * (q + 1) : 128 * (q + 2)], adjacent)
            at = TILES * half + q
            done = in_time(now, before, mask_ref[0, pl.ds(at, 1)], mask_ref[1, pl.ds(at, 1)])
            kept = kept_ref[q, slot]
            own = done[:16] + jnp.where(second_row, pltpu.roll(kept, 32, 1), 0.0)
            leave = done[16:] + jnp.where(second_row, kept, 0.0)
            out_ref[q, slot] = jnp.where(low_half, own, pltpu.roll(leave, 64, 1))
            out_ref[q + TILES, slot] = jnp.where(low_half, pltpu.roll(own, 64, 1), leave)
            before = now


def join2_kernel(parts_ref, out_ref):
    lane, _, _ = lanes()
    first_row, low_half = lane < 32, lane < 64

    def band(s):
        here, after = parts_ref[s], parts_ref[(s + 1) % SPACE]
        return jnp.where(
            first_row,
            pltpu.roll(here, 96, 1) + pltpu.roll(after, 64, 1),
            pltpu.roll(here, 64, 1) + pltpu.roll(after, 32, 1),
        )

    for p in range(16):
        tile = jnp.where(low_half, band(2 * p), pltpu.roll(band(2 * p + 1), 64, 1))
        for i in range(W * X):
            out_ref[i, p] = tile


def fold_kernel(qk_ref, value_ref, proj_ref, out_ref):
    scores = lax.dot_general(
        qk_ref[0], qk_ref[1], (((1,), (1,)), ((), ())), precision=highest, preferred_element_type=f32
    )
    out_ref[0] = scores * (1.0 / math.sqrt(256))
    out_ref[1] = jnp.dot(
        value_ref[...], proj_ref[...], precision=highest, preferred_element_type=f32
    )


def attend_kernel(
    place_ref, mine_ref, other_ref, gain_ref, folded_ref, same_ref, cross_ref,
    high_ref, low_ref,
):
    gain = column(gain_ref[2:3])
    half, core = place_ref[0], place_ref[3]

    def gathered(p):
        blocks = []
        for slot in range(2):
            for u in range(W):
                source = X * jnp.where(half == slot, u, 1 - u)
                for x in range(X):
                    mine, other = mine_ref[source + x, p], other_ref[source + x, p]
                    blocks.append(jnp.where(core == slot, mine, other))
        return jnp.concatenate(blocks, axis=0)

    rows = gathered(place_ref[5]).T
    normed = rows * lax.rsqrt(jnp.mean(rows * rows, axis=1, keepdims=True) + epsilon) * gain_ref[2:3]
    queries = dot3_stacked(*split(normed), *split(folded_ref[0]))
    for p in range(16):
        tile = gathered(p)
        normed = tile * lax.rsqrt(jnp.mean(tile * tile, axis=0, keepdims=True) + epsilon) * gain
        high, low = split(normed)
        high_ref[:, 128 * p : 128 * p + 128] = high
        low_ref[:, 128 * p : 128 * p + 128] = low
    scores = dot3_stacked(*split(queries), high_ref[...], low_ref[...])
    weights = jnp.exp(scores - jnp.max(scores, axis=1, keepdims=True))
    total = jnp.sum(weights, axis=1, keepdims=True)
    attended = dot3_stacked(*split(weights), high_ref[...], low_ref[...], ((1,), (1,))) / total
    result = rows + dot3_stacked(*split(attended), *split(folded_ref[1]))
    first_core = place_ref[4] == 0
    same_ref[...] = jnp.where(first_core, result[:64], result[64:])
    cross_ref[...] = jnp.where(first_core, result[64:], result[:64])


AWAY = ((8, 7), (-7, 6), (-6, 5), (-5, 4), (-4, 3), (-3, 2), (-2, 1), (-1, 0))


def offsets():
    table = np.zeros((W * X, W * X, CORES), np.int32)
    for home in range(W * X):
        def hops(chip):
            across = abs(chip % X - home % X)
            return abs(chip // X - home // X) + min(across, X - across)

        for rank, chip in enumerate(sorted(range(W * X), key=hops)):
            table[chip, home] = AWAY[rank]
    return table % (K * L)


def delivery(table):
    routes = ([], [])
    for i in range(W * X):
        for z in range(K * L):
            for c in range(CORES):
                source = (i * K * L + z) * CORES + c
                home, f = z % TILES, z // TILES
                chip = (z + int(table[i, home, c])) % (K * L)
                for route, core in zip(routes, (f, 1 - f)):
                    route.append((source, (home * K * L + chip) * CORES + core))
    return routes


def body(
    video,
    clip_ids,
    norm1_gain,
    conv1_weight,
    norm2_gain,
    conv2_weight,
    norm3_gain,
    qk_weight,
    value_weight,
    proj_weight,
):
    space = ("k", "l", "c")
    h, w, x, k, l, c = (lax.axis_index(n) for n in ("h", "w", "x", "k", "l", "c"))
    z, i = 2 * k + l, X * w + x
    table = offsets()
    rows_at = (z + jnp.asarray(table)[i, z % TILES, c]) % (K * L)
    place = jnp.stack([h, w, x, c, z // TILES, rows_at, CORES * z + c]).astype(jnp.int32)

    earlier = jnp.concatenate([jnp.full((2,), -1, jnp.int32), clip_ids])
    same = jnp.stack([earlier[1:-1] == clip_ids, earlier[:-2] == clip_ids]).astype(f32)
    masks = jnp.repeat(same, 64, axis=1).reshape(2, 16, 128)
    masks = jnp.concatenate([masks, jnp.zeros((2, 1, 128), f32)], axis=1)

    mirror = [(i, 3 - i) for i in range(H * W)]
    weight_1 = conv1_weight.reshape(432, 256)
    weight_2 = conv2_weight.reshape(432, 256)
    partner_1 = lax.ppermute(weight_1, ("h", "w"), mirror)
    partner_2 = lax.ppermute(weight_2, ("h", "w"), mirror)
    swap = [(0, 1), (1, 0)]
    gains = jnp.stack([norm1_gain, norm2_gain, norm3_gain])

    folded = call(fold_kernel, shape(2, 256, 256), [], qk_weight, value_weight, proj_weight)
    spread = call(spread_kernel, shape(W * X, 256, 128), [], video.reshape(128, 256))
    gathered = lax.all_to_all(spread, ("w", "x"), 0, 0)
    weights_scratch = [pltpu.VMEM((2, 432, 256), bf16)] * 2
    own, onward, kept = call(
        conv1_kernel,
        [shape(9, 2, 16, 128), shape(9, 2, 16, 128), shape(TILES, 2, 16, 128)],
        weights_scratch + [pltpu.VMEM((2, 432, 256), f32)],
        place,
        gathered.reshape(W * X, H * W, X, 16, 128),
        weight_1,
        partner_1,
        gains,
        masks,
        smem=1,
    )
    arrived = lax.ppermute(onward, space, [(i, (i + 1) % SPACE) for i in range(SPACE)])
    tiles, history = call(
        join1_kernel,
        [shape(8, 2, 16, 128), shape(2, 2, 16, 128)],
        [],
        place,
        own,
        arrived,
        smem=1,
    )
    history = lax.ppermute(history, ("h", "w"), mirror[: H * W // 2])
    second = call(send1_kernel, shape(W * X, TILES + 1, 2, 16, 128), [], tiles, history)
    second = lax.all_to_all(second, ("w", "x"), 0, 0)
    parts = call(
        conv2_kernel,
        shape(K * L, CORES, 16, 128),
        [pltpu.VMEM((256, 1152), bf16)] * 2 + [pltpu.VMEM((432, 1152), f32)],
        place,
        second,
        weight_2,
        partner_2,
        gains,
        masks,
        kept,
        smem=1,
    )
    parts = lax.all_to_all(parts.reshape(SPACE, 16, 128), space, 0, 0)
    frame = call(join2_kernel, shape(W * X, 16, 16, 128), [], parts)
    mine = lax.all_to_all(frame, ("w", "x"), 0, 0)
    other = lax.ppermute(mine, "c", swap)
    same_core, other_core = call(
        attend_kernel,
        [shape(64, 256), shape(64, 256)],
        [
            pltpu.VMEM((256, 2048), bf16),
            pltpu.VMEM((256, 2048), bf16),
        ],
        place,
        mine,
        other,
        gains,
        folded,
        smem=1,
    )
    route_0, route_1 = delivery(table)
    same_core = lax.ppermute(same_core, ("w", "x", "k", "l", "c"), route_0)
    other_core = lax.ppermute(other_core, ("w", "x", "k", "l", "c"), route_1)
    first_frame = jnp.where(c == 0, same_core, other_core)
    second_frame = jnp.where(c == 0, other_core, same_core)
    return jnp.stack([first_frame, second_frame]).reshape(video.shape)


def solution(mesh):
    grid = Mesh(mesh.devices.reshape(H, W, X, K, L, CORES), ("h", "w", "x", "k", "l", "c"))
    tm, space = ("h", "w", "x"), ("k", "l", "c")
    in_specs = (
        P(tm, space, None, None),
        P(),
        P(),
        P(None, None, None, tm, None),
        P(),
        P(None, None, None, tm, None),
        P(),
        P(),
        P(),
        P(),
    )
    return jax.shard_map(
        body, mesh=grid, in_specs=in_specs, out_specs=P(tm, space, None, None), check_vma=False
    )
```

```python
import math

import jax
import jax.numpy as jnp
import numpy as np
from jax import lax
from jax.experimental import pallas as pl
from jax.experimental.pallas import tpu as pltpu
from jax.sharding import Mesh
from jax.sharding import PartitionSpec as P

highest = lax.Precision.HIGHEST
epsilon = 1e-06
f32 = jnp.float32
bf16 = jnp.bfloat16

H, W, X, K, L, CORES = 2, 2, 4, 8, 2, 2
SPACE = K * L * CORES
TILES = 8

VMEM_LIMIT = 48 * 1024 * 1024


def call(kernel, out_shape, scratch, *operands, smem=0):
    return pl.pallas_call(
        kernel,
        out_shape=out_shape,
        in_specs=[pl.BlockSpec(memory_space=pltpu.SMEM)] * smem
        + [pl.BlockSpec(memory_space=pltpu.VMEM)] * (len(operands) - smem),
        out_specs=jax.tree.map(lambda _: pl.BlockSpec(memory_space=pltpu.VMEM), out_shape),
        scratch_shapes=scratch,
        compiler_params=pltpu.CompilerParams(vmem_limit_bytes=VMEM_LIMIT),
    )(*operands)


def shape(*dims):
    return jax.ShapeDtypeStruct(dims, f32)


def column(gain_row):
    return jnp.broadcast_to(gain_row, (128, gain_row.shape[1])).T


def split(value):
    high = value.astype(bf16)
    return high, (value - high.astype(f32)).astype(bf16)


def dot3(a_high, a_low, b_high, b_low, dims=((1,), (0,))):
    def one(a, b):
        return lax.dot_general(a, b, (dims, ((), ())), preferred_element_type=f32)

    return one(a_high, b_low) + one(a_low, b_high) + one(a_high, b_high)


def dot3_stacked(a_high, a_low, b_high, b_low, dims=((1,), (0,))):
    def one(a, b):
        return lax.dot_general(a, b, (dims, ((), ())), preferred_element_type=f32)

    rows = a_high.shape[0]
    both = one(jnp.concatenate([a_high, a_low], axis=0), b_high)
    return both[:rows] + (both[rows:] + one(a_high, b_low))


def norm_silu(value, gain):
    scale = lax.rsqrt(jnp.mean(value * value, axis=0, keepdims=True) + epsilon)
    value = value * scale * gain
    return value / (1.0 + jnp.exp(-value))


def lanes():
    lane = lax.broadcasted_iota(jnp.int32, (16, 128), 1)
    return lane, lane % 32, (lane // 32) % 2


def row_taps(product, a):
    _, across, _ = lanes()
    left, right = across >= 1, across <= 30
    rows = []
    for b in range(3):
        base = (a * 9 + b * 3) * 16
        rows.append(
            product[base + 16 : base + 32]
            + jnp.where(left, pltpu.roll(product[base : base + 16], 1, 1), 0.0)
            + jnp.where(right, pltpu.roll(product[base + 32 : base + 48], 127, 1), 0.0)
        )
    return rows


def taps_shifted(product):
    _, _, row = lanes()
    first_row = row == 0
    result = []
    for a in range(3):
        rows = row_taps(product, a)
        stay = rows[2] + jnp.where(first_row, 0.0, pltpu.roll(rows[1], 32, 1))
        go = rows[0] + jnp.where(first_row, pltpu.roll(rows[1], 96, 1), 0.0)
        result.append(jnp.concatenate([stay, go], axis=0))
    return result


def taps(product, adjacent):
    _, _, row = lanes()
    first_row = row == 0
    result = []
    for a in range(3):
        rows = row_taps(product, a)
        cross = jnp.where(first_row, rows[0], rows[2])
        cross = jnp.where(first_row, pltpu.roll(cross, 96, 1), pltpu.roll(cross, 32, 1))
        own = rows[1] + jnp.where(adjacent, cross, 0.0)
        leave = jnp.where(first_row, rows[2], rows[0])
        result.append(jnp.concatenate([own, leave], axis=0))
    return result


def in_time(now, before, mask_1, mask_2):
    lane = lax.broadcasted_iota(jnp.int32, (32, 128), 1)
    pair = jnp.where(lane < 64, now[1], before[1])
    return now[2] + mask_1 * pltpu.roll(pair, 64, 1) + mask_2 * before[0]


def spread_kernel(video_ref, out_ref):
    flipped = video_ref[...].T
    for i in range(W * X):
        out_ref[i] = flipped


def conv1_kernel(
    place_ref, video_ref, weight_ref, partner_ref, gain_ref, mask_ref,
    own_ref, onward_ref, last_ref, last_onward_ref, kept_ref, high_ref, low_ref, product_ref,
):
    gain = column(gain_ref[0:1])
    for g, ref in enumerate((weight_ref, partner_ref)):
        high_ref[g], low_ref[g] = split(ref[...])
    half, across = place_ref[0], place_ref[2]
    mine = 2 * half + place_ref[1]

    def finish(j, now, before):
        masks = mask_ref[0, pl.ds(8 * half + j, 1)], mask_ref[1, pl.ds(8 * half + j, 1)]
        for g in range(2):
            slot = half if g == 0 else 1 - half
            done = in_time(now[g], before[g], *masks)
            if j < TILES:
                own_ref[j, slot] = done[:16]
                onward_ref[j, slot] = done[16:]
            if j >= TILES - 1:
                last_ref[j - TILES + 1, slot] = done[:16]
                last_onward_ref[j - TILES + 1, slot] = done[16:]

    def step(p, before):
        pieces = []
        for side in range(2):
            j = 2 * p + side
            kept_ref[j, half] = video_ref[j, mine, across]
            kept_ref[j, 1 - half] = video_ref[j, 3 - mine, across]
            tile = video_ref[j].reshape(256, 128)
            pieces.append(split(norm_silu(tile, gain)))
        high = jnp.concatenate([pieces[0][0], pieces[1][0]], axis=1)
        low = jnp.concatenate([pieces[0][1], pieces[1][1]], axis=1)
        for g in range(2):
            product_ref[g] = dot3(high_ref[g], low_ref[g], high, low)
        for side in range(2):
            now = [taps_shifted(product_ref[g, :, 128 * side : 128 * side + 128]) for g in range(2)]
            finish(2 * p + side, now, before)
            before = now
        return before

    zeros = [[jnp.zeros((32, 128), f32)] * 3] * 2
    last = zeros
    for p in range(TILES // 2):
        last = step(p, last)
    finish(TILES, zeros, last)


def join1_kernel(
    place_ref, own_ref, arrived_ref, last_ref, last_arrived_ref, out_ref
):
    _, _, row = lanes()
    first_row = row == 0
    at_edge = place_ref[6] == 0

    def joined(own, arrived):
        return jnp.where(at_edge, jnp.where(first_row, arrived, own), own + arrived)

    for q in range(TILES + 1):
        for slot in range(2):
            if q == 0:
                tile = joined(last_ref[0, slot], last_arrived_ref[0, slot])
            else:
                tile = joined(own_ref[q - 1, slot], arrived_ref[q - 1, slot])
            if q == 1:
                tile = tile + joined(last_ref[1, slot], last_arrived_ref[1, slot])
            for i in range(W * X):
                out_ref[i, q, slot] = tile


def conv2_kernel(
    place_ref, second_ref, weight_ref, partner_ref, gain_ref, mask_ref, kept_ref,
    out_ref, high_ref, low_ref, product_ref,
):
    lane, _, row = lanes()
    low_half, first_row = lane < 64, row == 0
    adjacent = place_ref[6] != 0
    gain = column(gain_ref[1:2])
    half = place_ref[0]
    for q in range(TILES + 1):
        blocks = []
        for slot in range(2):
            for u in range(W):
                source = jnp.where(half == slot, u, 1 - u)
                blocks += [second_ref[X * source + x, q, slot] for x in range(X)]
        high, low = split(norm_silu(jnp.concatenate(blocks, axis=0), gain))
        high_ref[:, 128 * q : 128 * q + 128] = high
        low_ref[:, 128 * q : 128 * q + 128] = low
    for g, ref in enumerate((weight_ref, partner_ref)):
        slot = half if g == 0 else 1 - half
        w_high, w_low = split(ref[...])
        product_ref[...] = dot3(w_high, w_low, high_ref[...], low_ref[...])
        before = taps(product_ref[:, :128], adjacent)
        for q in range(TILES):
            now = taps(product_ref[:, 128 * (q + 1) : 128 * (q + 2)], adjacent)
            at = TILES * half + q
            done = in_time(now, before, mask_ref[0, pl.ds(at, 1)], mask_ref[1, pl.ds(at, 1)])
            own, leave = done[:16], done[16:]
            here = jnp.where(first_row, pltpu.roll(own, 96, 1), leave) + kept_ref[q, slot]
            above = jnp.where(first_row, leave, pltpu.roll(own, 32, 1))
            out_ref[q, slot] = jnp.where(low_half, here, pltpu.roll(above, 64, 1))
            out_ref[q + TILES, slot] = jnp.where(low_half, pltpu.roll(here, 64, 1), above)
            before = now


def join2_kernel(parts_ref, out_ref):
    lane, _, _ = lanes()
    low_half = lane < 64
    for p in range(16):
        outer = jnp.where(low_half, parts_ref[2 * p], parts_ref[(2 * p + 2) % SPACE])
        tile = outer + pltpu.roll(parts_ref[2 * p + 1], 64, 1)
        for i in range(W * X):
            out_ref[i, p] = tile


def fold_kernel(qk_ref, value_ref, proj_ref, out_ref):
    scores = lax.dot_general(
        qk_ref[0], qk_ref[1], (((1,), (1,)), ((), ())), precision=highest, preferred_element_type=f32
    )
    out_ref[0] = scores * (1.0 / math.sqrt(256))
    out_ref[1] = jnp.dot(
        value_ref[...], proj_ref[...], precision=highest, preferred_element_type=f32
    )


def attend_kernel(
    place_ref, mine_ref, other_ref, gain_ref, folded_ref, same_ref, cross_ref,
    high_ref, low_ref,
):
    gain = column(gain_ref[2:3])
    half, core = place_ref[0], place_ref[3]

    def gathered(p):
        blocks = []
        for slot in range(2):
            for u in range(W):
                source = X * jnp.where(half == slot, u, 1 - u)
                for x in range(X):
                    mine, other = mine_ref[source + x, p], other_ref[source + x, p]
                    blocks.append(jnp.where(core == slot, mine, other))
        return jnp.concatenate(blocks, axis=0)

    rows = gathered(place_ref[5]).T
    normed = rows * lax.rsqrt(jnp.mean(rows * rows, axis=1, keepdims=True) + epsilon) * gain_ref[2:3]
    queries = dot3_stacked(*split(normed), *split(folded_ref[0]))
    for p in range(16):
        tile = gathered(p)
        normed = tile * lax.rsqrt(jnp.mean(tile * tile, axis=0, keepdims=True) + epsilon) * gain
        high, low = split(normed)
        high_ref[:, 128 * p : 128 * p + 128] = high
        low_ref[:, 128 * p : 128 * p + 128] = low
    scores = dot3_stacked(*split(queries), high_ref[...], low_ref[...])
    weights = jnp.exp(scores - jnp.max(scores, axis=1, keepdims=True))
    total = jnp.sum(weights, axis=1, keepdims=True)
    attended = dot3_stacked(*split(weights), high_ref[...], low_ref[...], ((1,), (1,))) / total
    result = rows + dot3_stacked(*split(attended), *split(folded_ref[1]))
    first_core = place_ref[4] == 0
    same_ref[...] = jnp.where(first_core, result[:64], result[64:])
    cross_ref[...] = jnp.where(first_core, result[64:], result[:64])


AWAY = ((8, 7), (-7, 6), (-6, 5), (-5, 4), (-4, 3), (-3, 2), (-2, 1), (-1, 0))


def offsets():
    table = np.zeros((W * X, W * X, CORES), np.int32)
    for home in range(W * X):
        def hops(chip):
            across = abs(chip % X - home % X)
            return abs(chip // X - home // X) + min(across, X - across)

        for rank, chip in enumerate(sorted(range(W * X), key=hops)):
            table[chip, home] = AWAY[rank]
    return table % (K * L)


def delivery(table):
    routes = ([], [])
    for i in range(W * X):
        for z in range(K * L):
            for c in range(CORES):
                source = (i * K * L + z) * CORES + c
                home, f = z % TILES, z // TILES
                chip = (z + int(table[i, home, c])) % (K * L)
                for route, core in zip(routes, (f, 1 - f)):
                    route.append((source, (home * K * L + chip) * CORES + core))
    return routes


def body(
    video,
    clip_ids,
    norm1_gain,
    conv1_weight,
    norm2_gain,
    conv2_weight,
    norm3_gain,
    qk_weight,
    value_weight,
    proj_weight,
):
    space = ("k", "l", "c")
    h, w, x, k, l, c = (lax.axis_index(n) for n in ("h", "w", "x", "k", "l", "c"))
    z, i = 2 * k + l, X * w + x
    table = offsets()
    rows_at = (z + jnp.asarray(table)[i, z % TILES, c]) % (K * L)
    place = jnp.stack([h, w, x, c, z // TILES, rows_at, CORES * z + c]).astype(jnp.int32)

    earlier = jnp.concatenate([jnp.full((2,), -1, jnp.int32), clip_ids])
    same = jnp.stack([earlier[1:-1] == clip_ids, earlier[:-2] == clip_ids]).astype(f32)
    masks = jnp.repeat(same, 64, axis=1).reshape(2, 16, 128)
    masks = jnp.concatenate([masks, jnp.zeros((2, 1, 128), f32)], axis=1)

    mirror = [(i, 3 - i) for i in range(H * W)]
    weight_1 = conv1_weight.reshape(432, 256)
    weight_2 = conv2_weight.reshape(432, 256)
    partner_1 = lax.ppermute(weight_1, ("h", "w"), mirror)
    partner_2 = lax.ppermute(weight_2, ("h", "w"), mirror)
    swap = [(0, 1), (1, 0)]
    gains = jnp.stack([norm1_gain, norm2_gain, norm3_gain])

    folded = call(fold_kernel, shape(2, 256, 256), [], qk_weight, value_weight, proj_weight)
    spread = call(spread_kernel, shape(W * X, 256, 128), [], video.reshape(128, 256))
    gathered = lax.all_to_all(spread, ("w", "x"), 0, 0)
    weights_scratch = [pltpu.VMEM((2, 432, 256), bf16)] * 2
    own, onward, last, last_onward, kept = call(
        conv1_kernel,
        [
            shape(TILES, 2, 16, 128),
            shape(TILES, 2, 16, 128),
            shape(2, 2, 16, 128),
            shape(2, 2, 16, 128),
            shape(TILES, 2, 16, 128),
        ],
        weights_scratch + [pltpu.VMEM((2, 432, 256), f32)],
        place,
        gathered.reshape(W * X, H * W, X, 16, 128),
        weight_1,
        partner_1,
        gains,
        masks,
        smem=1,
    )
    onto_next = [
        (i * SPACE + s, j * SPACE + (s + 1) % SPACE)
        for i, j in mirror[: H * W // 2]
        for s in range(SPACE)
    ]
    last = lax.ppermute(last, ("h", "w"), mirror[: H * W // 2])
    last_arrived = lax.ppermute(last_onward, ("h", "w") + space, onto_next)
    arrived = lax.ppermute(onward, space, [(i, (i + 1) % SPACE) for i in range(SPACE)])
    second = call(
        join1_kernel,
        shape(W * X, TILES + 1, 2, 16, 128),
        [],
        place,
        own,
        arrived,
        last,
        last_arrived,
        smem=1,
    )
    second = lax.all_to_all(second, ("w", "x"), 0, 0)
    parts = call(
        conv2_kernel,
        shape(K * L, CORES, 16, 128),
        [pltpu.VMEM((256, 1152), bf16)] * 2 + [pltpu.VMEM((432, 1152), f32)],
        place,
        second,
        weight_2,
        partner_2,
        gains,
        masks,
        kept,
        smem=1,
    )
    parts = lax.all_to_all(parts.reshape(SPACE, 16, 128), space, 0, 0)
    frame = call(join2_kernel, shape(W * X, 16, 16, 128), [], parts)
    mine = lax.all_to_all(frame, ("w", "x"), 0, 0)
    other = lax.ppermute(mine, "c", swap)
    same_core, other_core = call(
        attend_kernel,
        [shape(64, 256), shape(64, 256)],
        [
            pltpu.VMEM((256, 2048), bf16),
            pltpu.VMEM((256, 2048), bf16),
        ],
        place,
        mine,
        other,
        gains,
        folded,
        smem=1,
    )
    route_0, route_1 = delivery(table)
    same_core = lax.ppermute(same_core, ("w", "x", "k", "l", "c"), route_0)
    other_core = lax.ppermute(other_core, ("w", "x", "k", "l", "c"), route_1)
    first_frame = jnp.where(c == 0, same_core, other_core)
    second_frame = jnp.where(c == 0, other_core, same_core)
    return jnp.stack([first_frame, second_frame]).reshape(video.shape)


def solution(mesh):
    grid = Mesh(mesh.devices.reshape(H, W, X, K, L, CORES), ("h", "w", "x", "k", "l", "c"))
    tm, space = ("h", "w", "x"), ("k", "l", "c")
    in_specs = (
        P(tm, space, None, None),
        P(),
        P(),
        P(None, None, None, tm, None),
        P(),
        P(None, None, None, tm, None),
        P(),
        P(),
        P(),
        P(),
    )
    return jax.shard_map(
        body, mesh=grid, in_specs=in_specs, out_specs=P(tm, space, None, None), check_vma=False
    )
```

```python
import math

import jax
import jax.numpy as jnp
import numpy as np
from jax import lax
from jax.experimental import pallas as pl
from jax.experimental.pallas import tpu as pltpu
from jax.sharding import Mesh
from jax.sharding import PartitionSpec as P

highest = lax.Precision.HIGHEST
epsilon = 1e-06
f32 = jnp.float32
bf16 = jnp.bfloat16

H, W, X, K, L, CORES = 2, 2, 4, 8, 2, 2
SPACE = K * L * CORES
TILES = 8

VMEM_LIMIT = 48 * 1024 * 1024


def call(kernel, out_shape, scratch, *operands, smem=0):
    return pl.pallas_call(
        kernel,
        out_shape=out_shape,
        in_specs=[pl.BlockSpec(memory_space=pltpu.SMEM)] * smem
        + [pl.BlockSpec(memory_space=pltpu.VMEM)] * (len(operands) - smem),
        out_specs=jax.tree.map(lambda _: pl.BlockSpec(memory_space=pltpu.VMEM), out_shape),
        scratch_shapes=scratch,
        compiler_params=pltpu.CompilerParams(vmem_limit_bytes=VMEM_LIMIT),
    )(*operands)


def shape(*dims):
    return jax.ShapeDtypeStruct(dims, f32)


def column(gain_row):
    return jnp.broadcast_to(gain_row, (128, gain_row.shape[1])).T


def split(value):
    high = value.astype(bf16)
    return high, (value - high.astype(f32)).astype(bf16)


def dot3(a_high, a_low, b_high, b_low, dims=((1,), (0,))):
    def one(a, b):
        return lax.dot_general(a, b, (dims, ((), ())), preferred_element_type=f32)

    return one(a_high, b_low) + one(a_low, b_high) + one(a_high, b_high)


def dot3_stacked(a_high, a_low, b_high, b_low, dims=((1,), (0,))):
    def one(a, b):
        return lax.dot_general(a, b, (dims, ((), ())), preferred_element_type=f32)

    rows = a_high.shape[0]
    both = one(jnp.concatenate([a_high, a_low], axis=0), b_high)
    return both[:rows] + (both[rows:] + one(a_high, b_low))


def norm_silu(value, gain):
    scale = lax.rsqrt(jnp.mean(value * value, axis=0, keepdims=True) + epsilon)
    value = value * scale * gain
    return value / (1.0 + jnp.exp(-value))


def lanes():
    lane = lax.broadcasted_iota(jnp.int32, (16, 128), 1)
    return lane, lane % 32, (lane // 32) % 2


def row_taps(product, a):
    _, across, _ = lanes()
    left, right = across >= 1, across <= 30
    rows = []
    for b in range(3):
        base = (a * 9 + b * 3) * 16
        rows.append(
            product[base + 16 : base + 32]
            + jnp.where(left, pltpu.roll(product[base : base + 16], 1, 1), 0.0)
            + jnp.where(right, pltpu.roll(product[base + 32 : base + 48], 127, 1), 0.0)
        )
    return rows


def taps(product, adjacent):
    _, _, row = lanes()
    first_row = row == 0
    result = []
    for a in range(3):
        above, same, below = row_taps(product, a)
        if adjacent is not None:
            below = jnp.where(first_row | adjacent, below, 0.0)
            above = jnp.where(first_row & ~adjacent, 0.0, above)
        stay = below + jnp.where(first_row, 0.0, pltpu.roll(same, 32, 1))
        go = above + jnp.where(first_row, pltpu.roll(same, 96, 1), 0.0)
        result.append(jnp.concatenate([stay, go], axis=0))
    return result


def in_time(now, before, mask_1, mask_2):
    lane = lax.broadcasted_iota(jnp.int32, (32, 128), 1)
    pair = jnp.where(lane < 64, now[1], before[1])
    return now[2] + mask_1 * pltpu.roll(pair, 64, 1) + mask_2 * before[0]


def spread_kernel(video_ref, out_ref):
    flipped = video_ref[...].T
    for i in range(W * X):
        out_ref[i] = flipped


def conv1_kernel(
    place_ref, video_ref, weight_ref, partner_ref, gain_ref, mask_ref,
    own_ref, onward_ref, last_ref, last_onward_ref, kept_ref, high_ref, low_ref, product_ref,
):
    gain = column(gain_ref[0:1])
    for g, ref in enumerate((weight_ref, partner_ref)):
        high_ref[g], low_ref[g] = split(ref[...])
    half, across = place_ref[0], place_ref[2]
    mine = 2 * half + place_ref[1]

    def finish(j, now, before):
        masks = mask_ref[0, pl.ds(8 * half + j, 1)], mask_ref[1, pl.ds(8 * half + j, 1)]
        for g in range(2):
            slot = half if g == 0 else 1 - half
            done = in_time(now[g], before[g], *masks)
            if j < TILES:
                own_ref[j, slot] = done[:16]
                onward_ref[j, slot] = done[16:]
            if j >= TILES - 1:
                last_ref[j - TILES + 1, slot] = done[:16]
                last_onward_ref[j - TILES + 1, slot] = done[16:]

    def step(p, before):
        pieces = []
        for side in range(2):
            j = 2 * p + side
            kept_ref[j, half] = video_ref[j, mine, across]
            kept_ref[j, 1 - half] = video_ref[j, 3 - mine, across]
            tile = video_ref[j].reshape(256, 128)
            pieces.append(split(norm_silu(tile, gain)))
        high = jnp.concatenate([pieces[0][0], pieces[1][0]], axis=1)
        low = jnp.concatenate([pieces[0][1], pieces[1][1]], axis=1)
        for g in range(2):
            product_ref[g] = dot3(high_ref[g], low_ref[g], high, low)
        for side in range(2):
            now = [taps(product_ref[g, :, 128 * side : 128 * side + 128], None) for g in range(2)]
            finish(2 * p + side, now, before)
            before = now
        return before

    zeros = [[jnp.zeros((32, 128), f32)] * 3] * 2
    last = zeros
    for p in range(TILES // 2):
        last = step(p, last)
    finish(TILES, zeros, last)


def join1_kernel(
    place_ref, own_ref, arrived_ref, last_ref, last_arrived_ref, out_ref
):
    _, _, row = lanes()
    first_row = row == 0
    at_edge = place_ref[6] == 0

    def joined(own, arrived):
        return jnp.where(at_edge, jnp.where(first_row, arrived, own), own + arrived)

    for q in range(TILES + 1):
        for slot in range(2):
            if q == 0:
                tile = joined(last_ref[0, slot], last_arrived_ref[0, slot])
            else:
                tile = joined(own_ref[q - 1, slot], arrived_ref[q - 1, slot])
            if q == 1:
                tile = tile + joined(last_ref[1, slot], last_arrived_ref[1, slot])
            for i in range(W * X):
                out_ref[i, q, slot] = tile


def conv2_kernel(
    place_ref, second_ref, weight_ref, partner_ref, gain_ref, mask_ref, kept_ref,
    stay_ref, go_ref, high_ref, low_ref, product_ref,
):
    adjacent = jnp.full((16, 128), place_ref[6], jnp.int32) != 0
    gain = column(gain_ref[1:2])
    half = place_ref[0]
    for q in range(TILES + 1):
        blocks = []
        for slot in range(2):
            for u in range(W):
                source = jnp.where(half == slot, u, 1 - u)
                blocks += [second_ref[X * source + x, q, slot] for x in range(X)]
        high, low = split(norm_silu(jnp.concatenate(blocks, axis=0), gain))
        high_ref[:, 128 * q : 128 * q + 128] = high
        low_ref[:, 128 * q : 128 * q + 128] = low
    for g, ref in enumerate((weight_ref, partner_ref)):
        slot = half if g == 0 else 1 - half
        w_high, w_low = split(ref[...])
        product_ref[...] = dot3(w_high, w_low, high_ref[...], low_ref[...])
        before = taps(product_ref[:, :128], adjacent)
        for q in range(TILES):
            now = taps(product_ref[:, 128 * (q + 1) : 128 * (q + 2)], adjacent)
            at = TILES * half + q
            done = in_time(now, before, mask_ref[0, pl.ds(at, 1)], mask_ref[1, pl.ds(at, 1)])
            stay_ref[q, slot] = done[:16]
            go_ref[q, slot] = done[16:] + kept_ref[q, slot]
            before = now


def join2_kernel(stay_ref, arrived_ref, out_ref):
    lane, _, _ = lanes()
    low_half = lane < 64
    for q in range(TILES):
        first, second = (stay_ref[q, slot] + arrived_ref[q, slot] for slot in range(2))
        out_ref[q] = jnp.where(low_half, first, pltpu.roll(second, 64, 1))
        out_ref[q + TILES] = jnp.where(low_half, pltpu.roll(first, 64, 1), second)


def pair_kernel(parts_ref, out_ref):
    lane, _, _ = lanes()
    low_half = lane < 64
    for m in range(8):
        first, second = parts_ref[2 * m], parts_ref[2 * m + 1]
        tiles = (
            jnp.where(low_half, first, pltpu.roll(second, 64, 1)),
            jnp.where(low_half, pltpu.roll(first, 64, 1), second),
        )
        for i in range(W * X):
            for slot in range(2):
                out_ref[i, m, slot] = tiles[slot]


def fold_kernel(qk_ref, value_ref, proj_ref, out_ref):
    scores = lax.dot_general(
        qk_ref[0], qk_ref[1], (((1,), (1,)), ((), ())), precision=highest, preferred_element_type=f32
    )
    out_ref[0] = scores * (1.0 / math.sqrt(256))
    out_ref[1] = jnp.dot(
        value_ref[...], proj_ref[...], precision=highest, preferred_element_type=f32
    )


def attend_kernel(
    place_ref, mine_ref, other_ref, gain_ref, folded_ref, same_ref, cross_ref,
    high_ref, low_ref,
):
    gain = column(gain_ref[2:3])
    half, core = place_ref[0], place_ref[3]

    def gathered(read):
        blocks = []
        for slot in range(2):
            for u in range(W):
                source = X * jnp.where(half == slot, u, 1 - u)
                blocks += [read(source + x, slot) for x in range(X)]
        return jnp.concatenate(blocks, axis=0)

    def of_core(which, m):
        return gathered(
            lambda source, slot: jnp.where(
                core == which, mine_ref[source, m, slot], other_ref[source, m, slot]
            )
        )

    even_at = place_ref[5]
    odd_at = (even_at + 1) & (K * L - 1)
    even, odd = of_core(1, even_at >> 1), of_core(0, odd_at >> 1)
    even = jnp.where((even_at & 1) == 0, even, pltpu.roll(even, 64, 1))
    odd = jnp.where((odd_at & 1) == 1, odd, pltpu.roll(odd, 64, 1))
    low_half = lax.broadcasted_iota(jnp.int32, even.shape, 1) < 64
    rows = jnp.where(low_half, even, odd).T
    normed = rows * lax.rsqrt(jnp.mean(rows * rows, axis=1, keepdims=True) + epsilon) * gain_ref[2:3]
    queries = dot3_stacked(*split(normed), *split(folded_ref[0]))
    for p in range(16):
        ref, m = (mine_ref, p) if p < 8 else (other_ref, p - 8)
        tile = gathered(lambda source, slot: ref[source, m, slot])
        normed = tile * lax.rsqrt(jnp.mean(tile * tile, axis=0, keepdims=True) + epsilon) * gain
        high, low = split(normed)
        high_ref[:, 128 * p : 128 * p + 128] = high
        low_ref[:, 128 * p : 128 * p + 128] = low
    scores = dot3_stacked(*split(queries), high_ref[...], low_ref[...])
    weights = jnp.exp(scores - jnp.max(scores, axis=1, keepdims=True))
    total = jnp.sum(weights, axis=1, keepdims=True)
    attended = dot3_stacked(*split(weights), high_ref[...], low_ref[...], ((1,), (1,))) / total
    result = rows + dot3_stacked(*split(attended), *split(folded_ref[1]))
    first_core = place_ref[4] == 0
    same_ref[...] = jnp.where(first_core, result[:64], result[64:])
    cross_ref[...] = jnp.where(first_core, result[64:], result[:64])


AWAY = ((8, 7), (-7, 6), (-6, 5), (-5, 4), (-4, 3), (-3, 2), (-2, 1), (-1, 0))


def offsets():
    table = np.zeros((W * X, W * X, CORES), np.int32)
    for home in range(W * X):
        def hops(chip):
            across = abs(chip % X - home % X)
            return abs(chip // X - home // X) + min(across, X - across)

        for rank, chip in enumerate(sorted(range(W * X), key=hops)):
            table[chip, home] = AWAY[rank]
    return table % (K * L)


def delivery(table):
    routes = ([], [])
    for i in range(W * X):
        for z in range(K * L):
            for c in range(CORES):
                source = (i * K * L + z) * CORES + c
                home, f = z % TILES, z // TILES
                chip = (z + int(table[i, home, c])) % (K * L)
                for route, core in zip(routes, (f, 1 - f)):
                    route.append((source, (home * K * L + chip) * CORES + core))
    return routes


def body(
    video,
    clip_ids,
    norm1_gain,
    conv1_weight,
    norm2_gain,
    conv2_weight,
    norm3_gain,
    qk_weight,
    value_weight,
    proj_weight,
):
    space = ("k", "l", "c")
    h, w, x, k, l, c = (lax.axis_index(n) for n in ("h", "w", "x", "k", "l", "c"))
    z, i = 2 * k + l, X * w + x
    table = offsets()
    rows_at = (z + jnp.asarray(table)[i, z % TILES, c]) % (K * L)
    place = jnp.stack([h, w, x, c, z // TILES, rows_at, CORES * z + c]).astype(jnp.int32)

    earlier = jnp.concatenate([jnp.full((2,), -1, jnp.int32), clip_ids])
    same = jnp.stack([earlier[1:-1] == clip_ids, earlier[:-2] == clip_ids]).astype(f32)
    masks = jnp.repeat(same, 64, axis=1).reshape(2, 16, 128)
    masks = jnp.concatenate([masks, jnp.zeros((2, 1, 128), f32)], axis=1)

    mirror = [(i, 3 - i) for i in range(H * W)]
    weight_1 = conv1_weight.reshape(432, 256)
    weight_2 = conv2_weight.reshape(432, 256)
    partner_1 = lax.ppermute(weight_1, ("h", "w"), mirror)
    partner_2 = lax.ppermute(weight_2, ("h", "w"), mirror)
    swap = [(0, 1), (1, 0)]
    gains = jnp.stack([norm1_gain, norm2_gain, norm3_gain])

    folded = call(fold_kernel, shape(2, 256, 256), [], qk_weight, value_weight, proj_weight)
    spread = call(spread_kernel, shape(W * X, 256, 128), [], video.reshape(128, 256))
    gathered = lax.all_to_all(spread, ("w", "x"), 0, 0)
    weights_scratch = [pltpu.VMEM((2, 432, 256), bf16)] * 2
    own, onward, last, last_onward, kept = call(
        conv1_kernel,
        [
            shape(TILES, 2, 16, 128),
            shape(TILES, 2, 16, 128),
            shape(2, 2, 16, 128),
            shape(2, 2, 16, 128),
            shape(TILES, 2, 16, 128),
        ],
        weights_scratch + [pltpu.VMEM((2, 432, 256), f32)],
        place,
        gathered.reshape(W * X, H * W, X, 16, 128),
        weight_1,
        partner_1,
        gains,
        masks,
        smem=1,
    )
    onto_next = [
        (i * SPACE + s, j * SPACE + (s + 1) % SPACE)
        for i, j in mirror[: H * W // 2]
        for s in range(SPACE)
    ]
    last = lax.ppermute(last, ("h", "w"), mirror[: H * W // 2])
    last_arrived = lax.ppermute(last_onward, ("h", "w") + space, onto_next)
    ring = [(i, (i + 1) % SPACE) for i in range(SPACE)]
    arrived = lax.ppermute(onward, space, ring)
    second = call(
        join1_kernel,
        shape(W * X, TILES + 1, 2, 16, 128),
        [],
        place,
        own,
        arrived,
        last,
        last_arrived,
        smem=1,
    )
    second = lax.all_to_all(second, ("w", "x"), 0, 0)
    stay, go = call(
        conv2_kernel,
        [shape(TILES, 2, 16, 128)] * 2,
        [pltpu.VMEM((256, 1152), bf16)] * 2 + [pltpu.VMEM((432, 1152), f32)],
        place,
        second,
        weight_2,
        partner_2,
        gains,
        masks,
        kept,
        smem=1,
    )
    arrived = lax.ppermute(go, space, ring)
    parts = call(join2_kernel, shape(K * L, 16, 128), [], stay, arrived)
    parts = lax.all_to_all(parts, ("k", "l"), 0, 0)
    frame = call(pair_kernel, shape(W * X, 8, 2, 16, 128), [], parts)
    mine = lax.all_to_all(frame, ("w", "x"), 0, 0)
    other = lax.ppermute(mine, "c", swap)
    same_core, other_core = call(
        attend_kernel,
        [shape(64, 256), shape(64, 256)],
        [
            pltpu.VMEM((256, 2048), bf16),
            pltpu.VMEM((256, 2048), bf16),
        ],
        place,
        mine,
        other,
        gains,
        folded,
        smem=1,
    )
    route_0, route_1 = delivery(table)
    same_core = lax.ppermute(same_core, ("w", "x", "k", "l", "c"), route_0)
    other_core = lax.ppermute(other_core, ("w", "x", "k", "l", "c"), route_1)
    first_frame = jnp.where(c == 0, same_core, other_core)
    second_frame = jnp.where(c == 0, other_core, same_core)
    return jnp.stack([first_frame, second_frame]).reshape(video.shape)


def solution(mesh):
    grid = Mesh(mesh.devices.reshape(H, W, X, K, L, CORES), ("h", "w", "x", "k", "l", "c"))
    tm, space = ("h", "w", "x"), ("k", "l", "c")
    in_specs = (
        P(tm, space, None, None),
        P(),
        P(),
        P(None, None, None, tm, None),
        P(),
        P(None, None, None, tm, None),
        P(),
        P(),
        P(),
        P(),
    )
    return jax.shard_map(
        body, mesh=grid, in_specs=in_specs, out_specs=P(tm, space, None, None), check_vma=False
    )
```

```python
import math

import jax
import jax.numpy as jnp
import numpy as np
from jax import lax
from jax.experimental import pallas as pl
from jax.experimental.pallas import tpu as pltpu
from jax.sharding import Mesh
from jax.sharding import PartitionSpec as P

highest = lax.Precision.HIGHEST
epsilon = 1e-06
f32 = jnp.float32
bf16 = jnp.bfloat16

H, W, X, K, L, CORES = 2, 2, 4, 8, 2, 2
SPACE = K * L * CORES
TILES = 8

VMEM_LIMIT = 48 * 1024 * 1024


def call(kernel, out_shape, scratch, *operands, smem=0):
    return pl.pallas_call(
        kernel,
        out_shape=out_shape,
        in_specs=[pl.BlockSpec(memory_space=pltpu.SMEM)] * smem
        + [pl.BlockSpec(memory_space=pltpu.VMEM)] * (len(operands) - smem),
        out_specs=jax.tree.map(lambda _: pl.BlockSpec(memory_space=pltpu.VMEM), out_shape),
        scratch_shapes=scratch,
        compiler_params=pltpu.CompilerParams(vmem_limit_bytes=VMEM_LIMIT),
    )(*operands)


def shape(*dims):
    return jax.ShapeDtypeStruct(dims, f32)


def column(gain_row):
    return jnp.broadcast_to(gain_row, (128, gain_row.shape[1])).T


def split(value):
    high = value.astype(bf16)
    return high, (value - high.astype(f32)).astype(bf16)


def dot3(a_high, a_low, b_high, b_low, dims=((1,), (0,))):
    def one(a, b):
        return lax.dot_general(a, b, (dims, ((), ())), preferred_element_type=f32)

    return one(a_high, b_low) + one(a_low, b_high) + one(a_high, b_high)


def dot3_stacked(a_high, a_low, b_high, b_low, dims=((1,), (0,))):
    def one(a, b):
        return lax.dot_general(a, b, (dims, ((), ())), preferred_element_type=f32)

    rows = a_high.shape[0]
    both = one(jnp.concatenate([a_high, a_low], axis=0), b_high)
    return both[:rows] + (both[rows:] + one(a_high, b_low))


def norm_silu(value, gain):
    scale = lax.rsqrt(jnp.mean(value * value, axis=0, keepdims=True) + epsilon)
    value = value * scale * gain
    return value / (1.0 + jnp.exp(-value))


def lanes():
    lane = lax.broadcasted_iota(jnp.int32, (16, 128), 1)
    return lane, lane % 32, (lane // 32) % 2


def row_taps(product, a):
    _, across, _ = lanes()
    left, right = across >= 1, across <= 30
    rows = []
    for b in range(3):
        base = (a * 9 + b * 3) * 16
        rows.append(
            product[base + 16 : base + 32]
            + jnp.where(left, pltpu.roll(product[base : base + 16], 1, 1), 0.0)
            + jnp.where(right, pltpu.roll(product[base + 32 : base + 48], 127, 1), 0.0)
        )
    return rows


def taps(product, adjacent):
    _, _, row = lanes()
    first_row = row == 0
    result = []
    for a in range(3):
        above, same, below = row_taps(product, a)
        if adjacent is not None:
            below = jnp.where(first_row | adjacent, below, 0.0)
            above = jnp.where(first_row & ~adjacent, 0.0, above)
        stay = below + jnp.where(first_row, 0.0, pltpu.roll(same, 32, 1))
        go = above + jnp.where(first_row, pltpu.roll(same, 96, 1), 0.0)
        result.append(jnp.concatenate([stay, go], axis=0))
    return result


def in_time(now, before, mask_1, mask_2):
    lane = lax.broadcasted_iota(jnp.int32, (32, 128), 1)
    pair = jnp.where(lane < 64, now[1], before[1])
    return now[2] + mask_1 * pltpu.roll(pair, 64, 1) + mask_2 * before[0]


def spread_kernel(video_ref, out_ref):
    flipped = video_ref[...].T
    for i in range(W * X):
        out_ref[i] = flipped


def conv1_kernel(
    place_ref, video_ref, weight_ref, partner_ref, gain_ref, mask_ref, _,
    own_ref, onward_ref, last_ref, last_onward_ref, kept_ref, high_ref, low_ref, product_ref,
):
    gain = column(gain_ref[0:1])
    for g, ref in enumerate((weight_ref, partner_ref)):
        high_ref[g], low_ref[g] = split(ref[...])
    half, across = place_ref[0], place_ref[2]
    mine = 2 * half + place_ref[1]

    def finish(j, now, before):
        masks = mask_ref[0, pl.ds(8 * half + j, 1)], mask_ref[1, pl.ds(8 * half + j, 1)]
        for g in range(2):
            slot = half if g == 0 else 1 - half
            done = in_time(now[g], before[g], *masks)
            if j < TILES:
                own_ref[j, slot] = done[:16]
                onward_ref[j, slot] = done[16:]
            if j >= TILES - 1:
                last_ref[j - TILES + 1, slot] = done[:16]
                last_onward_ref[j - TILES + 1, slot] = done[16:]

    def step(p, before):
        pieces = []
        for side in range(2):
            j = 2 * p + side
            kept_ref[j, half] = video_ref[j, mine, across]
            kept_ref[j, 1 - half] = video_ref[j, 3 - mine, across]
            tile = video_ref[j].reshape(256, 128)
            pieces.append(split(norm_silu(tile, gain)))
        high = jnp.concatenate([pieces[0][0], pieces[1][0]], axis=1)
        low = jnp.concatenate([pieces[0][1], pieces[1][1]], axis=1)
        for g in range(2):
            product_ref[g] = dot3(high_ref[g], low_ref[g], high, low)
        for side in range(2):
            now = [taps(product_ref[g, :, 128 * side : 128 * side + 128], None) for g in range(2)]
            finish(2 * p + side, now, before)
            before = now
        return before

    zeros = [[jnp.zeros((32, 128), f32)] * 3] * 2
    last = zeros
    for p in range(TILES // 2):
        last = step(p, last)
    finish(TILES, zeros, last)


def join1_kernel(
    place_ref, own_ref, arrived_ref, last_ref, last_arrived_ref, out_ref
):
    _, _, row = lanes()
    first_row = row == 0
    at_edge = place_ref[6] == 0

    def joined(own, arrived):
        return jnp.where(at_edge, jnp.where(first_row, arrived, own), own + arrived)

    for q in range(TILES + 1):
        for slot in range(2):
            if q == 0:
                tile = joined(last_ref[0, slot], last_arrived_ref[0, slot])
            else:
                tile = joined(own_ref[q - 1, slot], arrived_ref[q - 1, slot])
            if q == 1:
                tile = tile + joined(last_ref[1, slot], last_arrived_ref[1, slot])
            for i in range(W * X):
                out_ref[i, q, slot] = tile


def conv2_kernel(
    place_ref, second_ref, weight_ref, partner_ref, gain_ref, mask_ref, kept_ref,
    stay_ref, go_ref, high_ref, low_ref, product_ref,
):
    adjacent = jnp.full((16, 128), place_ref[6], jnp.int32) != 0
    gain = column(gain_ref[1:2])
    half = place_ref[0]
    for q in range(TILES + 1):
        blocks = []
        for slot in range(2):
            for u in range(W):
                source = jnp.where(half == slot, u, 1 - u)
                blocks += [second_ref[X * source + x, q, slot] for x in range(X)]
        high, low = split(norm_silu(jnp.concatenate(blocks, axis=0), gain))
        high_ref[:, 128 * q : 128 * q + 128] = high
        low_ref[:, 128 * q : 128 * q + 128] = low
    for g, ref in enumerate((weight_ref, partner_ref)):
        slot = half if g == 0 else 1 - half
        w_high, w_low = split(ref[...])
        product_ref[...] = dot3(w_high, w_low, high_ref[...], low_ref[...])
        before = taps(product_ref[:, :128], adjacent)
        for q in range(TILES):
            now = taps(product_ref[:, 128 * (q + 1) : 128 * (q + 2)], adjacent)
            at = TILES * half + q
            done = in_time(now, before, mask_ref[0, pl.ds(at, 1)], mask_ref[1, pl.ds(at, 1)])
            stay_ref[q, slot] = done[:16]
            go_ref[q, slot] = done[16:] + kept_ref[q, slot]
            before = now


def join2_kernel(stay_ref, arrived_ref, out_ref):
    lane, _, _ = lanes()
    low_half = lane < 64
    for q in range(TILES):
        first, second = (stay_ref[q, slot] + arrived_ref[q, slot] for slot in range(2))
        out_ref[q] = jnp.where(low_half, first, pltpu.roll(second, 64, 1))
        out_ref[q + TILES] = jnp.where(low_half, pltpu.roll(first, 64, 1), second)


def pair_kernel(parts_ref, out_ref):
    lane, _, _ = lanes()
    low_half = lane < 64
    for m in range(8):
        first, second = parts_ref[2 * m], parts_ref[2 * m + 1]
        tiles = (
            jnp.where(low_half, first, pltpu.roll(second, 64, 1)),
            jnp.where(low_half, pltpu.roll(first, 64, 1), second),
        )
        for i in range(W * X):
            for slot in range(2):
                out_ref[i, m, slot] = tiles[slot]


def fold_kernel(qk_ref, value_ref, proj_ref, out_ref):
    scores = lax.dot_general(
        qk_ref[0], qk_ref[1], (((1,), (1,)), ((), ())), precision=highest, preferred_element_type=f32
    )
    out_ref[0] = scores * (1.0 / math.sqrt(256))
    out_ref[1] = jnp.dot(
        value_ref[...], proj_ref[...], precision=highest, preferred_element_type=f32
    )


def gathered(place_ref, frame_ref, m):
    blocks = []
    for slot in range(2):
        for u in range(W):
            source = X * jnp.where(place_ref[0] == slot, u, 1 - u)
            blocks += [frame_ref[source + x, m, slot] for x in range(X)]
    return jnp.concatenate(blocks, axis=0)


def attend(place_ref, frame_ref, gain_ref, queries, high_ref, low_ref):
    gain = column(gain_ref[2:3])
    for m in range(8):
        tile = gathered(place_ref, frame_ref, m)
        normed = tile * lax.rsqrt(jnp.mean(tile * tile, axis=0, keepdims=True) + epsilon) * gain
        high, low = split(normed)
        high_ref[:, 128 * m : 128 * m + 128] = high
        low_ref[:, 128 * m : 128 * m + 128] = low
    scores = dot3_stacked(*split(queries), high_ref[...], low_ref[...])
    most = jnp.max(scores, axis=1, keepdims=True)
    weights = jnp.exp(scores - most)
    total = jnp.sum(weights, axis=1, keepdims=True)
    return most, total, dot3_stacked(*split(weights), high_ref[...], low_ref[...], ((1,), (1,)))


def attend_mine_kernel(
    place_ref, frame_ref, gain_ref, folded_ref,
    rows_ref, queries_ref, most_ref, total_ref, sum_ref, high_ref, low_ref,
):
    first_at, second_at = place_ref[4], place_ref[5]
    first = gathered(place_ref, frame_ref, first_at >> 1)
    second = gathered(place_ref, frame_ref, second_at >> 1)
    first = jnp.where((first_at & 1) == 0, first, pltpu.roll(first, 64, 1))
    second = jnp.where((second_at & 1) == 1, second, pltpu.roll(second, 64, 1))
    low_half = lax.broadcasted_iota(jnp.int32, first.shape, 1) < 64
    rows = jnp.where(low_half, first, second).T
    normed = rows * lax.rsqrt(jnp.mean(rows * rows, axis=1, keepdims=True) + epsilon) * gain_ref[2:3]
    queries = dot3_stacked(*split(normed), *split(folded_ref[0]))
    rows_ref[...] = rows
    queries_ref[...] = queries
    most, total, sum_ref[...] = attend(place_ref, frame_ref, gain_ref, queries, high_ref, low_ref)
    most_ref[...] = jnp.broadcast_to(most, (128, 128))
    total_ref[...] = jnp.broadcast_to(total, (128, 128))


def attend_other_kernel(
    place_ref, frame_ref, gain_ref, folded_ref, rows_ref, queries_ref, most_ref, total_ref, sum_ref,
    first_ref, second_ref, high_ref, low_ref,
):
    most, total, weighted = attend(
        place_ref, frame_ref, gain_ref, queries_ref[...], high_ref, low_ref
    )
    most_before, total_before = most_ref[:, 0:1], total_ref[:, 0:1]
    top = jnp.maximum(most, most_before)
    now, before = jnp.exp(most - top), jnp.exp(most_before - top)
    attended = (weighted * now + sum_ref[...] * before) / (total * now + total_before * before)
    result = rows_ref[...] + dot3_stacked(*split(attended), *split(folded_ref[1]))
    first_ref[...] = result[:64]
    second_ref[...] = result[64:]


AWAY = ((8, 7), (-6, -7), (6, 5), (-4, -5), (4, 3), (-2, -3), (2, 1), (0, -1))


def offsets():
    table = np.zeros((W * X, W * X, 2, 2), np.int32)
    for home in range(W * X):
        def hops(chip):
            across = abs(chip % X - home % X)
            return abs(chip // X - home // X) + min(across, X - across)

        for rank, chip in enumerate(sorted(range(W * X), key=hops)):
            table[chip, home] = AWAY[rank], AWAY[rank][::-1]
    return table % (K * L)


def delivery(table):
    routes = ([], [])
    for i in range(W * X):
        for z in range(K * L):
            for c in range(CORES):
                source = (i * K * L + z) * CORES + c
                home = z % TILES
                for band, route in enumerate(routes):
                    chip = (z + int(table[i, home, z // TILES, band])) % (K * L)
                    route.append((source, (home * K * L + chip) * CORES + 1 - c))
    return routes


def body(
    video,
    clip_ids,
    norm1_gain,
    conv1_weight,
    norm2_gain,
    conv2_weight,
    norm3_gain,
    qk_weight,
    value_weight,
    proj_weight,
):
    space = ("k", "l", "c")
    h, w, x, k, l, c = (lax.axis_index(n) for n in ("h", "w", "x", "k", "l", "c"))
    z, i = 2 * k + l, X * w + x
    table = offsets()
    bands_at = (z + jnp.asarray(table)[i, z % TILES, z // TILES] + 1 - c) % (K * L)
    place = jnp.stack([h, w, x, c, bands_at[0], bands_at[1], CORES * z + c]).astype(jnp.int32)

    earlier = jnp.concatenate([jnp.full((2,), -1, jnp.int32), clip_ids])
    same = jnp.stack([earlier[1:-1] == clip_ids, earlier[:-2] == clip_ids]).astype(f32)
    masks = jnp.repeat(same, 64, axis=1).reshape(2, 16, 128)
    masks = jnp.concatenate([masks, jnp.zeros((2, 1, 128), f32)], axis=1)

    mirror = [(i, 3 - i) for i in range(H * W)]
    weight_1 = conv1_weight.reshape(432, 256)
    weight_2 = conv2_weight.reshape(432, 256)
    partner_1 = lax.ppermute(weight_1, ("h", "w"), mirror)
    partner_2 = lax.ppermute(weight_2, ("h", "w"), mirror)
    swap = [(0, 1), (1, 0)]
    gains = jnp.stack([norm1_gain, norm2_gain, norm3_gain])

    folded = call(fold_kernel, shape(2, 256, 256), [], qk_weight, value_weight, proj_weight)
    spread = call(spread_kernel, shape(W * X, 256, 128), [], video.reshape(128, 256))
    gathered = lax.all_to_all(spread, ("w", "x"), 0, 0)
    weights_scratch = [pltpu.VMEM((2, 432, 256), bf16)] * 2
    own, onward, last, last_onward, kept = call(
        conv1_kernel,
        [
            shape(TILES, 2, 16, 128),
            shape(TILES, 2, 16, 128),
            shape(2, 2, 16, 128),
            shape(2, 2, 16, 128),
            shape(TILES, 2, 16, 128),
        ],
        weights_scratch + [pltpu.VMEM((2, 432, 256), f32)],
        place,
        gathered.reshape(W * X, H * W, X, 16, 128),
        weight_1,
        partner_1,
        gains,
        masks,
        folded,
        smem=1,
    )
    onto_next = [
        (i * SPACE + s, j * SPACE + (s + 1) % SPACE)
        for i, j in mirror[: H * W // 2]
        for s in range(SPACE)
    ]
    last = lax.ppermute(last, ("h", "w"), mirror[: H * W // 2])
    last_arrived = lax.ppermute(last_onward, ("h", "w") + space, onto_next)
    ring = [(i, (i + 1) % SPACE) for i in range(SPACE)]
    arrived = lax.ppermute(onward, space, ring)
    second = call(
        join1_kernel,
        shape(W * X, TILES + 1, 2, 16, 128),
        [],
        place,
        own,
        arrived,
        last,
        last_arrived,
        smem=1,
    )
    second = lax.all_to_all(second, ("w", "x"), 0, 0)
    stay, go = call(
        conv2_kernel,
        [shape(TILES, 2, 16, 128)] * 2,
        [pltpu.VMEM((256, 1152), bf16)] * 2 + [pltpu.VMEM((432, 1152), f32)],
        place,
        second,
        weight_2,
        partner_2,
        gains,
        masks,
        kept,
        smem=1,
    )
    arrived = lax.ppermute(go, space, ring)
    parts = call(join2_kernel, shape(K * L, 16, 128), [], stay, arrived)
    parts = lax.all_to_all(parts, ("k", "l"), 0, 0)
    frame = call(pair_kernel, shape(W * X, 8, 2, 16, 128), [], parts)
    mine = lax.all_to_all(frame, ("w", "x"), 0, 0)
    other = lax.ppermute(mine, "c", swap)
    halves = [pltpu.VMEM((256, 1024), bf16)] * 2
    partial = call(
        attend_mine_kernel,
        [shape(128, 256), shape(128, 256), shape(128, 128), shape(128, 128), shape(128, 256)],
        halves,
        place,
        mine,
        gains,
        folded,
        smem=1,
    )
    near, far = call(
        attend_other_kernel,
        [shape(64, 256), shape(64, 256)],
        halves,
        place,
        other,
        gains,
        folded,
        *partial,
        smem=1,
    )
    route_near, route_far = delivery(table)
    near = lax.ppermute(near, ("w", "x", "k", "l", "c"), route_near)
    far = lax.ppermute(far, ("w", "x", "k", "l", "c"), route_far)
    from_first = (z + i) % 2 == 0
    first_frame = jnp.where(from_first, near, far)
    second_frame = jnp.where(from_first, far, near)
    return jnp.stack([first_frame, second_frame]).reshape(video.shape)


def solution(mesh):
    grid = Mesh(mesh.devices.reshape(H, W, X, K, L, CORES), ("h", "w", "x", "k", "l", "c"))
    tm, space = ("h", "w", "x"), ("k", "l", "c")
    in_specs = (
        P(tm, space, None, None),
        P(),
        P(),
        P(None, None, None, tm, None),
        P(),
        P(None, None, None, tm, None),
        P(),
        P(),
        P(),
        P(),
    )
    return jax.shard_map(
        body, mesh=grid, in_specs=in_specs, out_specs=P(tm, space, None, None), check_vma=False
    )
```

```python
import math

import jax
import jax.numpy as jnp
import numpy as np
from jax import lax
from jax.experimental import pallas as pl
from jax.experimental.pallas import tpu as pltpu
from jax.sharding import Mesh
from jax.sharding import PartitionSpec as P

highest = lax.Precision.HIGHEST
epsilon = 1e-06
f32 = jnp.float32
bf16 = jnp.bfloat16

H, W, X, K, L, CORES = 2, 2, 4, 8, 2, 2
SPACE = K * L * CORES
TILES = 8

VMEM_LIMIT = 48 * 1024 * 1024


def call(kernel, out_shape, scratch, *operands, smem=0):
    return pl.pallas_call(
        kernel,
        out_shape=out_shape,
        in_specs=[pl.BlockSpec(memory_space=pltpu.SMEM)] * smem
        + [pl.BlockSpec(memory_space=pltpu.VMEM)] * (len(operands) - smem),
        out_specs=jax.tree.map(lambda _: pl.BlockSpec(memory_space=pltpu.VMEM), out_shape),
        scratch_shapes=scratch,
        compiler_params=pltpu.CompilerParams(vmem_limit_bytes=VMEM_LIMIT),
    )(*operands)


def shape(*dims):
    return jax.ShapeDtypeStruct(dims, f32)


def column(gain_row):
    return jnp.broadcast_to(gain_row, (128, gain_row.shape[1])).T


def split(value):
    high = value.astype(bf16)
    return high, (value - high.astype(f32)).astype(bf16)


def dot3(a_high, a_low, b_high, b_low, dims=((1,), (0,))):
    def one(a, b):
        return lax.dot_general(a, b, (dims, ((), ())), preferred_element_type=f32)

    return one(a_high, b_low) + one(a_low, b_high) + one(a_high, b_high)


def dot3_stacked(a_high, a_low, b_high, b_low, dims=((1,), (0,))):
    def one(a, b):
        return lax.dot_general(a, b, (dims, ((), ())), preferred_element_type=f32)

    rows = a_high.shape[0]
    both = one(jnp.concatenate([a_high, a_low], axis=0), b_high)
    return both[:rows] + (both[rows:] + one(a_high, b_low))


def split3(value):
    high = value.astype(bf16)
    rest = value - high.astype(f32)
    middle = rest.astype(bf16)
    return high, middle, (rest - middle.astype(f32)).astype(bf16)


def dot6(a, b):
    def one(parts, right):
        return jnp.dot(jnp.concatenate(parts, axis=0), right, preferred_element_type=f32)

    rows = a[0].shape[0]
    by_high, by_middle, by_low = one(a, b[0]), one(a[:2], b[1]), one(a[:1], b[2])
    small = by_high[2 * rows :] + (by_middle[rows:] + by_low)
    return by_high[:rows] + (by_high[rows : 2 * rows] + by_middle[:rows] + small)


def norm_silu(value, gain):
    scale = lax.rsqrt(jnp.mean(value * value, axis=0, keepdims=True) + epsilon)
    value = value * scale * gain
    return value / (1.0 + jnp.exp(-value))


def lanes():
    lane = lax.broadcasted_iota(jnp.int32, (16, 128), 1)
    return lane, lane % 32, (lane // 32) % 2


def row_taps(product, a):
    _, across, _ = lanes()
    left, right = across >= 1, across <= 30
    rows = []
    for b in range(3):
        base = (a * 9 + b * 3) * 16
        rows.append(
            product[base + 16 : base + 32]
            + jnp.where(left, pltpu.roll(product[base : base + 16], 1, 1), 0.0)
            + jnp.where(right, pltpu.roll(product[base + 32 : base + 48], 127, 1), 0.0)
        )
    return rows


def taps(product, adjacent):
    _, _, row = lanes()
    first_row = row == 0
    result = []
    for a in range(3):
        above, same, below = row_taps(product, a)
        if adjacent is not None:
            below = jnp.where(first_row | adjacent, below, 0.0)
            above = jnp.where(first_row & ~adjacent, 0.0, above)
        stay = below + jnp.where(first_row, 0.0, pltpu.roll(same, 32, 1))
        go = above + jnp.where(first_row, pltpu.roll(same, 96, 1), 0.0)
        result.append(jnp.concatenate([stay, go], axis=0))
    return result


def in_time(now, before, mask_1, mask_2):
    lane = lax.broadcasted_iota(jnp.int32, (32, 128), 1)
    pair = jnp.where(lane < 64, now[1], before[1])
    return now[2] + mask_1 * pltpu.roll(pair, 64, 1) + mask_2 * before[0]


def spread_kernel(video_ref, out_ref):
    flipped = video_ref[...].T
    for i in range(W * X):
        out_ref[i] = flipped


def conv1_kernel(
    place_ref, video_ref, weight_ref, partner_ref, gain_ref, mask_ref, _,
    own_ref, onward_ref, last_ref, last_onward_ref, kept_ref, high_ref, low_ref, product_ref,
):
    gain = column(gain_ref[0:1])
    for g, ref in enumerate((weight_ref, partner_ref)):
        high_ref[g], low_ref[g] = split(ref[...])
    half, across = place_ref[0], place_ref[2]
    mine = 2 * half + place_ref[1]

    def finish(j, now, before):
        masks = mask_ref[0, pl.ds(8 * half + j, 1)], mask_ref[1, pl.ds(8 * half + j, 1)]
        for g in range(2):
            slot = half if g == 0 else 1 - half
            done = in_time(now[g], before[g], *masks)
            if j < TILES:
                own_ref[j, slot] = done[:16]
                onward_ref[j, slot] = done[16:]
            if j >= TILES - 1:
                last_ref[j - TILES + 1, slot] = done[:16]
                last_onward_ref[j - TILES + 1, slot] = done[16:]

    def step(p, before):
        pieces = []
        for side in range(2):
            j = 2 * p + side
            kept_ref[j, half] = video_ref[j, mine, across]
            kept_ref[j, 1 - half] = video_ref[j, 3 - mine, across]
            tile = video_ref[j].reshape(256, 128)
            pieces.append(split(norm_silu(tile, gain)))
        high = jnp.concatenate([pieces[0][0], pieces[1][0]], axis=1)
        low = jnp.concatenate([pieces[0][1], pieces[1][1]], axis=1)
        for g in range(2):
            product_ref[g] = dot3(high_ref[g], low_ref[g], high, low)
        for side in range(2):
            now = [taps(product_ref[g, :, 128 * side : 128 * side + 128], None) for g in range(2)]
            finish(2 * p + side, now, before)
            before = now
        return before

    zeros = [[jnp.zeros((32, 128), f32)] * 3] * 2
    last = zeros
    for p in range(TILES // 2):
        last = step(p, last)
    finish(TILES, zeros, last)


def join1_kernel(
    place_ref, own_ref, arrived_ref, last_ref, last_arrived_ref, out_ref
):
    _, _, row = lanes()
    first_row = row == 0
    at_edge = place_ref[6] == 0

    def joined(own, arrived):
        return jnp.where(at_edge, jnp.where(first_row, arrived, own), own + arrived)

    for q in range(TILES + 1):
        for slot in range(2):
            if q == 0:
                tile = joined(last_ref[0, slot], last_arrived_ref[0, slot])
            else:
                tile = joined(own_ref[q - 1, slot], arrived_ref[q - 1, slot])
            if q == 1:
                tile = tile + joined(last_ref[1, slot], last_arrived_ref[1, slot])
            for i in range(W * X):
                out_ref[i, q, slot] = tile


def conv2_kernel(
    place_ref, second_ref, weight_ref, partner_ref, gain_ref, mask_ref, kept_ref,
    stay_ref, go_ref, high_ref, low_ref, product_ref,
):
    adjacent = jnp.full((16, 128), place_ref[6], jnp.int32) != 0
    gain = column(gain_ref[1:2])
    half = place_ref[0]
    for q in range(TILES + 1):
        blocks = []
        for slot in range(2):
            for u in range(W):
                source = jnp.where(half == slot, u, 1 - u)
                blocks += [second_ref[X * source + x, q, slot] for x in range(X)]
        high, low = split(norm_silu(jnp.concatenate(blocks, axis=0), gain))
        high_ref[:, 128 * q : 128 * q + 128] = high
        low_ref[:, 128 * q : 128 * q + 128] = low
    for g, ref in enumerate((weight_ref, partner_ref)):
        slot = half if g == 0 else 1 - half
        w_high, w_low = split(ref[...])
        product_ref[...] = dot3(w_high, w_low, high_ref[...], low_ref[...])
        before = taps(product_ref[:, :128], adjacent)
        for q in range(TILES):
            now = taps(product_ref[:, 128 * (q + 1) : 128 * (q + 2)], adjacent)
            at = TILES * half + q
            done = in_time(now, before, mask_ref[0, pl.ds(at, 1)], mask_ref[1, pl.ds(at, 1)])
            stay_ref[q, slot] = done[:16]
            go_ref[q, slot] = done[16:] + kept_ref[q, slot]
            before = now


def join2_kernel(stay_ref, arrived_ref, out_ref):
    lane, _, _ = lanes()
    low_half = lane < 64
    for q in range(TILES):
        first, second = (stay_ref[q, slot] + arrived_ref[q, slot] for slot in range(2))
        out_ref[q] = jnp.where(low_half, first, pltpu.roll(second, 64, 1))
        out_ref[q + TILES] = jnp.where(low_half, pltpu.roll(first, 64, 1), second)


def pair_kernel(parts_ref, out_ref):
    lane, _, _ = lanes()
    low_half = lane < 64
    for m in range(8):
        first, second = parts_ref[2 * m], parts_ref[2 * m + 1]
        tiles = (
            jnp.where(low_half, first, pltpu.roll(second, 64, 1)),
            jnp.where(low_half, pltpu.roll(first, 64, 1), second),
        )
        for i in range(W * X):
            for slot in range(2):
                out_ref[i, m, slot] = tiles[slot]


def fold_kernel(qk_ref, value_ref, proj_ref, out_ref):
    scores = lax.dot_general(
        qk_ref[0], qk_ref[1], (((1,), (1,)), ((), ())), precision=highest, preferred_element_type=f32
    )
    out_ref[0] = scores * (1.0 / math.sqrt(256))
    out_ref[1] = jnp.dot(
        value_ref[...], proj_ref[...], precision=highest, preferred_element_type=f32
    )


def gathered(place_ref, frame_ref, m):
    blocks = []
    for slot in range(2):
        for u in range(W):
            source = X * jnp.where(place_ref[0] == slot, u, 1 - u)
            blocks += [frame_ref[source + x, m, slot] for x in range(X)]
    return jnp.concatenate(blocks, axis=0)


def attend(place_ref, frame_ref, gain_ref, queries, high_ref, middle_ref, low_ref):
    gain = column(gain_ref[2:3])
    for m in range(8):
        tile = gathered(place_ref, frame_ref, m)
        normed = tile * lax.rsqrt(jnp.mean(tile * tile, axis=0, keepdims=True) + epsilon) * gain
        for ref, piece in zip((high_ref, middle_ref, low_ref), split3(normed)):
            ref[:, 128 * m : 128 * m + 128] = piece
    scores = dot6(split3(queries), (high_ref[...], middle_ref[...], low_ref[...]))
    most = jnp.max(scores, axis=1, keepdims=True)
    weights = jnp.exp(scores - most)
    total = jnp.sum(weights, axis=1, keepdims=True)
    return most, total, dot3_stacked(*split(weights), high_ref[...], middle_ref[...], ((1,), (1,)))


def attend_mine_kernel(
    place_ref, frame_ref, gain_ref, folded_ref,
    rows_ref, queries_ref, most_ref, total_ref, sum_ref, high_ref, middle_ref, low_ref,
):
    first_at, second_at = place_ref[4], place_ref[5]
    first = gathered(place_ref, frame_ref, first_at >> 1)
    second = gathered(place_ref, frame_ref, second_at >> 1)
    first = jnp.where((first_at & 1) == 0, first, pltpu.roll(first, 64, 1))
    second = jnp.where((second_at & 1) == 1, second, pltpu.roll(second, 64, 1))
    low_half = lax.broadcasted_iota(jnp.int32, first.shape, 1) < 64
    rows = jnp.where(low_half, first, second).T
    normed = rows * lax.rsqrt(jnp.mean(rows * rows, axis=1, keepdims=True) + epsilon) * gain_ref[2:3]
    queries = dot6(split3(normed), split3(folded_ref[0]))
    rows_ref[...] = rows
    queries_ref[...] = queries
    most, total, sum_ref[...] = attend(
        place_ref, frame_ref, gain_ref, queries, high_ref, middle_ref, low_ref
    )
    most_ref[...] = jnp.broadcast_to(most, (128, 128))
    total_ref[...] = jnp.broadcast_to(total, (128, 128))


def attend_other_kernel(
    place_ref, frame_ref, gain_ref, folded_ref, rows_ref, queries_ref, most_ref, total_ref, sum_ref,
    first_ref, second_ref, high_ref, middle_ref, low_ref,
):
    most, total, weighted = attend(
        place_ref, frame_ref, gain_ref, queries_ref[...], high_ref, middle_ref, low_ref
    )
    most_before, total_before = most_ref[:, 0:1], total_ref[:, 0:1]
    top = jnp.maximum(most, most_before)
    now, before = jnp.exp(most - top), jnp.exp(most_before - top)
    attended = (weighted * now + sum_ref[...] * before) / (total * now + total_before * before)
    result = rows_ref[...] + dot3_stacked(*split(attended), *split(folded_ref[1]))
    first_ref[...] = result[:64]
    second_ref[...] = result[64:]


AWAY = ((8, 7), (-6, -7), (6, 5), (-4, -5), (4, 3), (-2, -3), (2, 1), (0, -1))


def offsets():
    table = np.zeros((W * X, W * X, 2, 2), np.int32)
    for home in range(W * X):
        def hops(chip):
            across = abs(chip % X - home % X)
            return abs(chip // X - home // X) + min(across, X - across)

        for rank, chip in enumerate(sorted(range(W * X), key=hops)):
            table[chip, home] = AWAY[rank], AWAY[rank][::-1]
    return table % (K * L)


def delivery(table):
    routes = ([], [])
    for i in range(W * X):
        for z in range(K * L):
            for c in range(CORES):
                source = (i * K * L + z) * CORES + c
                home = z % TILES
                for band, route in enumerate(routes):
                    chip = (z + int(table[i, home, z // TILES, band])) % (K * L)
                    route.append((source, (home * K * L + chip) * CORES + 1 - c))
    return routes


def body(
    video,
    clip_ids,
    norm1_gain,
    conv1_weight,
    norm2_gain,
    conv2_weight,
    norm3_gain,
    qk_weight,
    value_weight,
    proj_weight,
):
    space = ("k", "l", "c")
    h, w, x, k, l, c = (lax.axis_index(n) for n in ("h", "w", "x", "k", "l", "c"))
    z, i = 2 * k + l, X * w + x
    table = offsets()
    bands_at = (z + jnp.asarray(table)[i, z % TILES, z // TILES] + 1 - c) % (K * L)
    place = jnp.stack([h, w, x, c, bands_at[0], bands_at[1], CORES * z + c]).astype(jnp.int32)

    earlier = jnp.concatenate([jnp.full((2,), -1, jnp.int32), clip_ids])
    same = jnp.stack([earlier[1:-1] == clip_ids, earlier[:-2] == clip_ids]).astype(f32)
    masks = jnp.repeat(same, 64, axis=1).reshape(2, 16, 128)
    masks = jnp.concatenate([masks, jnp.zeros((2, 1, 128), f32)], axis=1)

    mirror = [(i, 3 - i) for i in range(H * W)]
    weight_1 = conv1_weight.reshape(432, 256)
    weight_2 = conv2_weight.reshape(432, 256)
    partner_1 = lax.ppermute(weight_1, ("h", "w"), mirror)
    partner_2 = lax.ppermute(weight_2, ("h", "w"), mirror)
    swap = [(0, 1), (1, 0)]
    gains = jnp.stack([norm1_gain, norm2_gain, norm3_gain])

    folded = call(fold_kernel, shape(2, 256, 256), [], qk_weight, value_weight, proj_weight)
    spread = call(spread_kernel, shape(W * X, 256, 128), [], video.reshape(128, 256))
    gathered = lax.all_to_all(spread, ("w", "x"), 0, 0)
    weights_scratch = [pltpu.VMEM((2, 432, 256), bf16)] * 2
    own, onward, last, last_onward, kept = call(
        conv1_kernel,
        [
            shape(TILES, 2, 16, 128),
            shape(TILES, 2, 16, 128),
            shape(2, 2, 16, 128),
            shape(2, 2, 16, 128),
            shape(TILES, 2, 16, 128),
        ],
        weights_scratch + [pltpu.VMEM((2, 432, 256), f32)],
        place,
        gathered.reshape(W * X, H * W, X, 16, 128),
        weight_1,
        partner_1,
        gains,
        masks,
        folded,
        smem=1,
    )
    onto_next = [
        (i * SPACE + s, j * SPACE + (s + 1) % SPACE)
        for i, j in mirror[: H * W // 2]
        for s in range(SPACE)
    ]
    last = lax.ppermute(last, ("h", "w"), mirror[: H * W // 2])
    last_arrived = lax.ppermute(last_onward, ("h", "w") + space, onto_next)
    ring = [(i, (i + 1) % SPACE) for i in range(SPACE)]
    arrived = lax.ppermute(onward, space, ring)
    second = call(
        join1_kernel,
        shape(W * X, TILES + 1, 2, 16, 128),
        [],
        place,
        own,
        arrived,
        last,
        last_arrived,
        smem=1,
    )
    second = lax.all_to_all(second, ("w", "x"), 0, 0)
    stay, go = call(
        conv2_kernel,
        [shape(TILES, 2, 16, 128)] * 2,
        [pltpu.VMEM((256, 1152), bf16)] * 2 + [pltpu.VMEM((432, 1152), f32)],
        place,
        second,
        weight_2,
        partner_2,
        gains,
        masks,
        kept,
        smem=1,
    )
    arrived = lax.ppermute(go, space, ring)
    parts = call(join2_kernel, shape(K * L, 16, 128), [], stay, arrived)
    parts = lax.all_to_all(parts, ("k", "l"), 0, 0)
    frame = call(pair_kernel, shape(W * X, 8, 2, 16, 128), [], parts)
    mine = lax.all_to_all(frame, ("w", "x"), 0, 0)
    other = lax.ppermute(mine, "c", swap)
    halves = [pltpu.VMEM((256, 1024), bf16)] * 3
    partial = call(
        attend_mine_kernel,
        [shape(128, 256), shape(128, 256), shape(128, 128), shape(128, 128), shape(128, 256)],
        halves,
        place,
        mine,
        gains,
        folded,
        smem=1,
    )
    near, far = call(
        attend_other_kernel,
        [shape(64, 256), shape(64, 256)],
        halves,
        place,
        other,
        gains,
        folded,
        *partial,
        smem=1,
    )
    route_near, route_far = delivery(table)
    near = lax.ppermute(near, ("w", "x", "k", "l", "c"), route_near)
    far = lax.ppermute(far, ("w", "x", "k", "l", "c"), route_far)
    from_first = (z + i) % 2 == 0
    first_frame = jnp.where(from_first, near, far)
    second_frame = jnp.where(from_first, far, near)
    return jnp.stack([first_frame, second_frame]).reshape(video.shape)


def solution(mesh):
    grid = Mesh(mesh.devices.reshape(H, W, X, K, L, CORES), ("h", "w", "x", "k", "l", "c"))
    tm, space = ("h", "w", "x"), ("k", "l", "c")
    in_specs = (
        P(tm, space, None, None),
        P(),
        P(),
        P(None, None, None, tm, None),
        P(),
        P(None, None, None, tm, None),
        P(),
        P(),
        P(),
        P(),
    )
    return jax.shard_map(
        body, mesh=grid, in_specs=in_specs, out_specs=P(tm, space, None, None), check_vma=False
    )
```

```python
import math

import jax
import jax.numpy as jnp
import numpy as np
from jax import lax
from jax.experimental import pallas as pl
from jax.experimental.pallas import tpu as pltpu
from jax.sharding import Mesh
from jax.sharding import PartitionSpec as P

highest = lax.Precision.HIGHEST
epsilon = 1e-06
f32 = jnp.float32
bf16 = jnp.bfloat16

H, W, X, K, L, CORES = 2, 2, 4, 8, 2, 2
SPACE = K * L * CORES
TILES = 8

VMEM_LIMIT = 48 * 1024 * 1024


def call(kernel, out_shape, scratch, *operands, smem=0):
    return pl.pallas_call(
        kernel,
        out_shape=out_shape,
        in_specs=[pl.BlockSpec(memory_space=pltpu.SMEM)] * smem
        + [pl.BlockSpec(memory_space=pltpu.VMEM)] * (len(operands) - smem),
        out_specs=jax.tree.map(lambda _: pl.BlockSpec(memory_space=pltpu.VMEM), out_shape),
        scratch_shapes=scratch,
        compiler_params=pltpu.CompilerParams(vmem_limit_bytes=VMEM_LIMIT),
    )(*operands)


def shape(*dims):
    return jax.ShapeDtypeStruct(dims, f32)


def column(gain_row):
    return jnp.broadcast_to(gain_row, (128, gain_row.shape[1])).T


def split(value):
    high = value.astype(bf16)
    return high, (value - high.astype(f32)).astype(bf16)


def dot3(a_high, a_low, b_high, b_low, dims=((1,), (0,))):
    def one(a, b):
        return lax.dot_general(a, b, (dims, ((), ())), preferred_element_type=f32)

    return one(a_high, b_low) + one(a_low, b_high) + one(a_high, b_high)


def dot3_stacked(a_high, a_low, b_high, b_low, dims=((1,), (0,))):
    def one(a, b):
        return lax.dot_general(a, b, (dims, ((), ())), preferred_element_type=f32)

    rows = a_high.shape[0]
    both = one(jnp.concatenate([a_high, a_low], axis=0), b_high)
    return both[:rows] + (both[rows:] + one(a_high, b_low))


def split3(value):
    high = value.astype(bf16)
    rest = value - high.astype(f32)
    middle = rest.astype(bf16)
    return high, middle, (rest - middle.astype(f32)).astype(bf16)


def dot6(a, b):
    def one(parts, right):
        return jnp.dot(jnp.concatenate(parts, axis=0), right, preferred_element_type=f32)

    rows = a[0].shape[0]
    by_high, by_middle, by_low = one(a, b[0]), one(a[:2], b[1]), one(a[:1], b[2])
    small = by_high[2 * rows :] + (by_middle[rows:] + by_low)
    return by_high[:rows] + (by_high[rows : 2 * rows] + by_middle[:rows] + small)


def norm_silu(value, gain):
    scale = lax.rsqrt(jnp.mean(value * value, axis=0, keepdims=True) + epsilon)
    value = value * scale * gain
    return value / (1.0 + jnp.exp(-value))


def lanes():
    lane = lax.broadcasted_iota(jnp.int32, (16, 128), 1)
    return lane, lane % 32, (lane // 32) % 2


def row_taps(product, a):
    _, across, _ = lanes()
    left, right = across >= 1, across <= 30
    rows = []
    for b in range(3):
        base = (a * 9 + b * 3) * 16
        rows.append(
            product[base + 16 : base + 32]
            + jnp.where(left, pltpu.roll(product[base : base + 16], 1, 1), 0.0)
            + jnp.where(right, pltpu.roll(product[base + 32 : base + 48], 127, 1), 0.0)
        )
    return rows


def taps(product, adjacent):
    _, _, row = lanes()
    first_row = row == 0
    result = []
    for a in range(3):
        above, same, below = row_taps(product, a)
        if adjacent is not None:
            below = jnp.where(first_row | adjacent, below, 0.0)
            above = jnp.where(first_row & ~adjacent, 0.0, above)
        stay = below + jnp.where(first_row, 0.0, pltpu.roll(same, 32, 1))
        go = above + jnp.where(first_row, pltpu.roll(same, 96, 1), 0.0)
        result.append(jnp.concatenate([stay, go], axis=0))
    return result


def in_time(now, before, mask_1, mask_2):
    lane = lax.broadcasted_iota(jnp.int32, (32, 128), 1)
    pair = jnp.where(lane < 64, now[1], before[1])
    return now[2] + mask_1 * pltpu.roll(pair, 64, 1) + mask_2 * before[0]


def spread_kernel(video_ref, out_ref):
    flipped = video_ref[...].T
    for i in range(W * X):
        out_ref[i] = flipped


def conv1_kernel(
    place_ref, video_ref, weight_ref, partner_ref, gain_ref, mask_ref, _,
    own_ref, onward_ref, last_ref, last_onward_ref, kept_ref, high_ref, low_ref, product_ref,
):
    gain = column(gain_ref[0:1])
    for g, ref in enumerate((weight_ref, partner_ref)):
        high_ref[g], low_ref[g] = split(ref[...])
    half, across = place_ref[0], place_ref[2]
    mine = 2 * half + place_ref[1]

    def finish(j, now, before):
        masks = mask_ref[0, pl.ds(8 * half + j, 1)], mask_ref[1, pl.ds(8 * half + j, 1)]
        for g in range(2):
            slot = half if g == 0 else 1 - half
            done = in_time(now[g], before[g], *masks)
            if j < TILES:
                own_ref[j, slot] = done[:16]
                onward_ref[j, slot] = done[16:]
            if j >= TILES - 1:
                last_ref[j - TILES + 1, slot] = done[:16]
                last_onward_ref[j - TILES + 1, slot] = done[16:]

    def step(p, before):
        pieces = []
        for side in range(2):
            j = 2 * p + side
            kept_ref[j, half] = video_ref[j, mine, across]
            kept_ref[j, 1 - half] = video_ref[j, 3 - mine, across]
            tile = video_ref[j].reshape(256, 128)
            pieces.append(split(norm_silu(tile, gain)))
        high = jnp.concatenate([pieces[0][0], pieces[1][0]], axis=1)
        low = jnp.concatenate([pieces[0][1], pieces[1][1]], axis=1)
        for g in range(2):
            product_ref[g] = dot3(high_ref[g], low_ref[g], high, low)
        for side in range(2):
            now = [taps(product_ref[g, :, 128 * side : 128 * side + 128], None) for g in range(2)]
            finish(2 * p + side, now, before)
            before = now
        return before

    zeros = [[jnp.zeros((32, 128), f32)] * 3] * 2
    last = zeros
    for p in range(TILES // 2):
        last = step(p, last)
    finish(TILES, zeros, last)


def join1_kernel(
    place_ref, own_ref, arrived_ref, last_ref, last_arrived_ref, out_ref
):
    _, _, row = lanes()
    first_row = row == 0
    at_edge = place_ref[6] == 0

    def joined(own, arrived):
        return jnp.where(at_edge, jnp.where(first_row, arrived, own), own + arrived)

    for q in range(TILES + 1):
        for slot in range(2):
            if q == 0:
                tile = joined(last_ref[0, slot], last_arrived_ref[0, slot])
            else:
                tile = joined(own_ref[q - 1, slot], arrived_ref[q - 1, slot])
            if q == 1:
                tile = tile + joined(last_ref[1, slot], last_arrived_ref[1, slot])
            for i in range(W * X):
                out_ref[i, q, slot] = tile


def conv2_kernel(
    place_ref, second_ref, weight_ref, partner_ref, gain_ref, mask_ref, kept_ref,
    stay_ref, go_ref, high_ref, low_ref, product_ref,
):
    adjacent = jnp.full((16, 128), place_ref[6], jnp.int32) != 0
    gain = column(gain_ref[1:2])
    half = place_ref[0]
    for g, ref in enumerate((weight_ref, partner_ref)):
        high_ref[g], low_ref[g] = split(ref[...])
    before = None
    for pair in range(0, TILES + 1, 2):
        tiles = range(pair, min(pair + 2, TILES + 1))
        pieces = []
        for q in tiles:
            blocks = []
            for slot in range(2):
                for u in range(W):
                    source = jnp.where(half == slot, u, 1 - u)
                    blocks += [second_ref[X * source + x, q, slot] for x in range(X)]
            pieces.append(split(norm_silu(jnp.concatenate(blocks, axis=0), gain)))
        high, low = (jnp.concatenate([p[i] for p in pieces], axis=1) for i in range(2))
        for g in range(2):
            product_ref[g, :, : 128 * len(tiles)] = dot3(high_ref[g], low_ref[g], high, low)
        for side, q in enumerate(tiles):
            now = [
                taps(product_ref[g, :, 128 * side : 128 * side + 128], adjacent) for g in range(2)
            ]
            if q > 0:
                at = TILES * half + q - 1
                masks = mask_ref[0, pl.ds(at, 1)], mask_ref[1, pl.ds(at, 1)]
                for g in range(2):
                    slot = half if g == 0 else 1 - half
                    done = in_time(now[g], before[g], *masks)
                    stay_ref[q - 1, slot] = done[:16]
                    go_ref[q - 1, slot] = done[16:] + kept_ref[q - 1, slot]
            before = now


def join2_kernel(stay_ref, arrived_ref, out_ref):
    lane, _, _ = lanes()
    low_half = lane < 64
    for q in range(TILES):
        first, second = (stay_ref[q, slot] + arrived_ref[q, slot] for slot in range(2))
        out_ref[q] = jnp.where(low_half, first, pltpu.roll(second, 64, 1))
        out_ref[q + TILES] = jnp.where(low_half, pltpu.roll(first, 64, 1), second)


def pair_kernel(parts_ref, out_ref):
    lane, _, _ = lanes()
    low_half = lane < 64
    for m in range(8):
        first, second = parts_ref[2 * m], parts_ref[2 * m + 1]
        tiles = (
            jnp.where(low_half, first, pltpu.roll(second, 64, 1)),
            jnp.where(low_half, pltpu.roll(first, 64, 1), second),
        )
        for i in range(W * X):
            for slot in range(2):
                out_ref[i, m, slot] = tiles[slot]


def fold_kernel(qk_ref, value_ref, proj_ref, out_ref):
    scores = lax.dot_general(
        qk_ref[0], qk_ref[1], (((1,), (1,)), ((), ())), precision=highest, preferred_element_type=f32
    )
    out_ref[0] = scores * (1.0 / math.sqrt(256))
    out_ref[1] = jnp.dot(
        value_ref[...], proj_ref[...], precision=highest, preferred_element_type=f32
    )


def gathered(place_ref, frame_ref, m):
    blocks = []
    for slot in range(2):
        for u in range(W):
            source = X * jnp.where(place_ref[0] == slot, u, 1 - u)
            blocks += [frame_ref[source + x, m, slot] for x in range(X)]
    return jnp.concatenate(blocks, axis=0)


def attend(place_ref, frame_ref, gain_ref, queries, high_ref, middle_ref, low_ref):
    gain = column(gain_ref[2:3])
    for m in range(8):
        tile = gathered(place_ref, frame_ref, m)
        normed = tile * lax.rsqrt(jnp.mean(tile * tile, axis=0, keepdims=True) + epsilon) * gain
        for ref, piece in zip((high_ref, middle_ref, low_ref), split3(normed)):
            ref[:, 128 * m : 128 * m + 128] = piece
    scores = dot6(split3(queries), (high_ref[...], middle_ref[...], low_ref[...]))
    most = jnp.max(scores, axis=1, keepdims=True)
    weights = jnp.exp(scores - most)
    total = jnp.sum(weights, axis=1, keepdims=True)
    return most, total, dot3_stacked(*split(weights), high_ref[...], middle_ref[...], ((1,), (1,)))


def attend_mine_kernel(
    place_ref, frame_ref, gain_ref, folded_ref,
    rows_ref, queries_ref, most_ref, total_ref, sum_ref, high_ref, middle_ref, low_ref,
):
    first_at, second_at = place_ref[4], place_ref[5]
    first = gathered(place_ref, frame_ref, first_at >> 1)
    second = gathered(place_ref, frame_ref, second_at >> 1)
    first = jnp.where((first_at & 1) == 0, first, pltpu.roll(first, 64, 1))
    second = jnp.where((second_at & 1) == 1, second, pltpu.roll(second, 64, 1))
    low_half = lax.broadcasted_iota(jnp.int32, first.shape, 1) < 64
    rows = jnp.where(low_half, first, second).T
    normed = rows * lax.rsqrt(jnp.mean(rows * rows, axis=1, keepdims=True) + epsilon) * gain_ref[2:3]
    queries = dot6(split3(normed), split3(folded_ref[0]))
    rows_ref[...] = rows
    queries_ref[...] = queries
    most, total, sum_ref[...] = attend(
        place_ref, frame_ref, gain_ref, queries, high_ref, middle_ref, low_ref
    )
    most_ref[...] = jnp.broadcast_to(most, (128, 128))
    total_ref[...] = jnp.broadcast_to(total, (128, 128))


def attend_other_kernel(
    place_ref, frame_ref, gain_ref, folded_ref, rows_ref, queries_ref, most_ref, total_ref, sum_ref,
    first_ref, second_ref, high_ref, middle_ref, low_ref,
):
    most, total, weighted = attend(
        place_ref, frame_ref, gain_ref, queries_ref[...], high_ref, middle_ref, low_ref
    )
    most_before, total_before = most_ref[:, 0:1], total_ref[:, 0:1]
    top = jnp.maximum(most, most_before)
    now, before = jnp.exp(most - top), jnp.exp(most_before - top)
    attended = (weighted * now + sum_ref[...] * before) / (total * now + total_before * before)
    result = rows_ref[...] + dot3_stacked(*split(attended), *split(folded_ref[1]))
    first_ref[...] = result[:64]
    second_ref[...] = result[64:]


AWAY = ((8, 7), (-6, -7), (6, 5), (-4, -5), (4, 3), (-2, -3), (2, 1), (0, -1))


def offsets():
    table = np.zeros((W * X, W * X, 2, 2), np.int32)
    for home in range(W * X):
        def hops(chip):
            across = abs(chip % X - home % X)
            return abs(chip // X - home // X) + min(across, X - across)

        for rank, chip in enumerate(sorted(range(W * X), key=hops)):
            table[chip, home] = AWAY[rank], AWAY[rank][::-1]
    return table % (K * L)


def delivery(table):
    routes = ([], [])
    for i in range(W * X):
        for z in range(K * L):
            for c in range(CORES):
                source = (i * K * L + z) * CORES + c
                home = z % TILES
                for band, route in enumerate(routes):
                    chip = (z + int(table[i, home, z // TILES, band])) % (K * L)
                    route.append((source, (home * K * L + chip) * CORES + 1 - c))
    return routes


def body(
    video,
    clip_ids,
    norm1_gain,
    conv1_weight,
    norm2_gain,
    conv2_weight,
    norm3_gain,
    qk_weight,
    value_weight,
    proj_weight,
):
    space = ("k", "l", "c")
    h, w, x, k, l, c = (lax.axis_index(n) for n in ("h", "w", "x", "k", "l", "c"))
    z, i = 2 * k + l, X * w + x
    table = offsets()
    bands_at = (z + jnp.asarray(table)[i, z % TILES, z // TILES] + 1 - c) % (K * L)
    place = jnp.stack([h, w, x, c, bands_at[0], bands_at[1], CORES * z + c]).astype(jnp.int32)

    earlier = jnp.concatenate([jnp.full((2,), -1, jnp.int32), clip_ids])
    same = jnp.stack([earlier[1:-1] == clip_ids, earlier[:-2] == clip_ids]).astype(f32)
    masks = jnp.repeat(same, 64, axis=1).reshape(2, 16, 128)
    masks = jnp.concatenate([masks, jnp.zeros((2, 1, 128), f32)], axis=1)

    mirror = [(i, 3 - i) for i in range(H * W)]
    weight_1 = conv1_weight.reshape(432, 256)
    weight_2 = conv2_weight.reshape(432, 256)
    partner_1 = lax.ppermute(weight_1, ("h", "w"), mirror)
    partner_2 = lax.ppermute(weight_2, ("h", "w"), mirror)
    swap = [(0, 1), (1, 0)]
    gains = jnp.stack([norm1_gain, norm2_gain, norm3_gain])

    folded = call(fold_kernel, shape(2, 256, 256), [], qk_weight, value_weight, proj_weight)
    spread = call(spread_kernel, shape(W * X, 256, 128), [], video.reshape(128, 256))
    gathered = lax.all_to_all(spread, ("w", "x"), 0, 0)
    weights_scratch = [pltpu.VMEM((2, 432, 256), bf16)] * 2
    own, onward, last, last_onward, kept = call(
        conv1_kernel,
        [
            shape(TILES, 2, 16, 128),
            shape(TILES, 2, 16, 128),
            shape(2, 2, 16, 128),
            shape(2, 2, 16, 128),
            shape(TILES, 2, 16, 128),
        ],
        weights_scratch + [pltpu.VMEM((2, 432, 256), f32)],
        place,
        gathered.reshape(W * X, H * W, X, 16, 128),
        weight_1,
        partner_1,
        gains,
        masks,
        folded,
        smem=1,
    )
    onto_next = [
        (i * SPACE + s, j * SPACE + (s + 1) % SPACE)
        for i, j in mirror[: H * W // 2]
        for s in range(SPACE)
    ]
    last = lax.ppermute(last, ("h", "w"), mirror[: H * W // 2])
    last_arrived = lax.ppermute(last_onward, ("h", "w") + space, onto_next)
    ring = [(i, (i + 1) % SPACE) for i in range(SPACE)]
    arrived = lax.ppermute(onward, space, ring)
    second = call(
        join1_kernel,
        shape(W * X, TILES + 1, 2, 16, 128),
        [],
        place,
        own,
        arrived,
        last,
        last_arrived,
        smem=1,
    )
    second = lax.all_to_all(second, ("w", "x"), 0, 0)
    stay, go = call(
        conv2_kernel,
        [shape(TILES, 2, 16, 128)] * 2,
        weights_scratch + [pltpu.VMEM((2, 432, 256), f32)],
        place,
        second,
        weight_2,
        partner_2,
        gains,
        masks,
        kept,
        smem=1,
    )
    arrived = lax.ppermute(go, space, ring)
    parts = call(join2_kernel, shape(K * L, 16, 128), [], stay, arrived)
    parts = lax.all_to_all(parts, ("k", "l"), 0, 0)
    frame = call(pair_kernel, shape(W * X, 8, 2, 16, 128), [], parts)
    mine = lax.all_to_all(frame, ("w", "x"), 0, 0)
    other = lax.ppermute(mine, "c", swap)
    halves = [pltpu.VMEM((256, 1024), bf16)] * 3
    partial = call(
        attend_mine_kernel,
        [shape(128, 256), shape(128, 256), shape(128, 128), shape(128, 128), shape(128, 256)],
        halves,
        place,
        mine,
        gains,
        folded,
        smem=1,
    )
    near, far = call(
        attend_other_kernel,
        [shape(64, 256), shape(64, 256)],
        halves,
        place,
        other,
        gains,
        folded,
        *partial,
        smem=1,
    )
    route_near, route_far = delivery(table)
    near = lax.ppermute(near, ("w", "x", "k", "l", "c"), route_near)
    far = lax.ppermute(far, ("w", "x", "k", "l", "c"), route_far)
    from_first = (z + i) % 2 == 0
    first_frame = jnp.where(from_first, near, far)
    second_frame = jnp.where(from_first, far, near)
    return jnp.stack([first_frame, second_frame]).reshape(video.shape)


def solution(mesh):
    grid = Mesh(mesh.devices.reshape(H, W, X, K, L, CORES), ("h", "w", "x", "k", "l", "c"))
    tm, space = ("h", "w", "x"), ("k", "l", "c")
    in_specs = (
        P(tm, space, None, None),
        P(),
        P(),
        P(None, None, None, tm, None),
        P(),
        P(None, None, None, tm, None),
        P(),
        P(),
        P(),
        P(),
    )
    return jax.shard_map(
        body, mesh=grid, in_specs=in_specs, out_specs=P(tm, space, None, None), check_vma=False
    )
```
